512 devices in a mesh: ka: 8 (over x, core), dev: 64 (over z, y).
Axes of the slice: x: 4, y: 4, z: 16, core: 2. Of those that a mesh axis runs over, the one named last changes fastest.
Arguments:
- density: float32 [4096, 2048], P('dev'), may hold values from 0 to 1
- fields_fwd: bfloat16 [8, 6, 4096, 2048], P('ka', None, 'dev'), may hold values from -0.796875 to 0.796875
- fields_adj: bfloat16 [8, 6, 4096, 2048], P('ka', None, 'dev'), may hold values from -0.796875 to 0.796875
- filter_band: float32 [4096, 17], replicated, may hold values from 0.2 to 1
- k_weights: float32 [8], replicated, may hold values from 0.3 to 3
- kpoint_ids: int32 [8], replicated, may hold values from 0 to 7, each once
Outputs:
- projected: float32 [4096, 2048], P('dev')
- design_grad: float32 [4096, 2048], P('dev')
The draws below stay inside these ranges and needn't reach their ends.
All inputs are finite; a program needn't handle non-finite values.
Results may differ from the reference program's by a relative error of at most 0.0003.
Values sent between devices are 32-bit elements; how exact they have to be, the bound alone decides.
A program may use at most 64 MiB of HBM per device.

```python
import math
import jax
import jax.numpy as jnp
from jax import lax

COLS = 2048
KPTS = 8
NROWS = 4096
TAPS = 17


def block_levels(rng, dims, shards, smallest, top_value):
    level, own = 1.0, jax.random.fold_in(rng, 6)
    for dim, blocks in shards:
        draws = jnp.exp(jax.random.uniform(jax.random.fold_in(own, dim), (blocks,), jnp.float32, smallest / len(shards), top_value / len(shards)))
        level = level * jnp.repeat(draws, dims[dim] // blocks).reshape([-1 if axis == dim else 1 for axis in range(len(dims))])
    return level


def bell_draw(stream_key, dims, spread, limit, pieces=(), kind=jnp.bfloat16):
    values = spread * jax.random.normal(stream_key, dims, jnp.float32)
    if pieces:
        values = values * block_levels(stream_key, dims, pieces, -0.22, 0.18)
    return jnp.clip(values, -limit, limit).astype(kind)


def setup_inputs(seed: int = 0) -> dict:
    splits = jax.random.split(jax.random.key(seed), 7)
    density = jnp.clip(1.0 * jax.random.uniform(splits[0], (NROWS, COLS), jnp.float32) ** block_levels(splits[0], (NROWS, COLS), ((0, 64),), -0.2, 0.2), 0.0, 1.0)
    fields_fwd = bell_draw(splits[1], (KPTS, 6, NROWS, COLS), 0.1, 0.796875, ((0, 8), (2, 64)))
    fields_adj = bell_draw(splits[2], (KPTS, 6, NROWS, COLS), 0.1, 0.796875, ((0, 8), (2, 64)))
    filter_band = jnp.clip(jax.random.uniform(splits[3], (NROWS, TAPS), jnp.float32, 0.2, 1.0), 0.2, 1.0)
    k_weights = jnp.clip(jnp.exp(jax.random.uniform(splits[4], (KPTS,), jnp.float32, math.log(0.3), math.log(3.0))), 0.3, 3.0)
    kpoint_ids = jax.random.permutation(splits[5], KPTS).astype(jnp.int32)
    return {"density": density, "fields_fwd": fields_fwd, "fields_adj": fields_adj, "filter_band": filter_band, "k_weights": k_weights, "kpoint_ids": kpoint_ids}


def normalize(filter_band):
    return filter_band / jnp.sum(filter_band, axis=1, keepdims=True)


def project(filtered):
    beta = 8.0
    eta = 0.5
    quot = jnp.tanh(beta * eta) + jnp.tanh(beta * (1.0 - eta))
    inner = jnp.tanh(beta * (filtered - eta))
    return (jnp.tanh(beta * eta) + inner) / quot, beta * (1.0 - inner * inner) / quot


def reference(density, fields_fwd, fields_adj, filter_band, k_weights, kpoint_ids):
    band = normalize(filter_band)
    nrows = density.shape[0]
    taps = band.shape[1]
    radius = (taps - 1) // 2
    padded = jnp.pad(density, ((radius, radius), (0, 0)))
    filtered = jnp.zeros_like(density)
    for j in range(taps):
        filtered = filtered + band[:, j][:, None] * padded[j:j + nrows]
    projected, slope = project(filtered)
    slots = jnp.arange(k_weights.shape[0], dtype=jnp.int32)
    weight = jnp.sum((kpoint_ids[:, None] == slots[None, :]).astype(jnp.float32) * k_weights[None, :], axis=1)

    def one_k(carry, item):
        fwd, adj, wk = item
        prod = fwd.astype(jnp.float32) * adj.astype(jnp.float32)
        term = jnp.sum(prod[0:3], axis=0) - jnp.sum(prod[3:6], axis=0)
        return carry + wk * term, 0

    sens, _ = lax.scan(one_k, jnp.zeros_like(density), (fields_fwd, fields_adj, weight))
    grad_filtered = 11.1 * slope * sens
    gpad = jnp.pad(grad_filtered, ((radius, radius), (0, 0)))
    bpad = jnp.pad(band, ((radius, radius), (0, 0)))
    design_grad = jnp.zeros_like(density)
    for j in range(taps):
        lo = 2 * radius - j
        design_grad = design_grad + bpad[lo:lo + nrows, j][:, None] * gpad[lo:lo + nrows]
    return projected, design_grad
```

```python
import functools

import jax
import jax.numpy as jnp
from jax import lax
from jax.experimental import pallas as pl
from jax.experimental.pallas import tpu as pltpu
from jax.sharding import PartitionSpec as P

MESH = pl.DeviceIdType.MESH
BETA, ETA = 8.0, 0.5


def split(value):
    high = value.astype(jnp.bfloat16)
    low = (value - high.astype(jnp.float32)).astype(jnp.bfloat16)
    return high, low


def kernel(
    sizes,
    density, fwd, adj, band_t, weights, ids,
    projected, design,
    fwd_buf, adj_buf, ext, band_buf, band_rows, mat, mat_t, inner_buf, weight_buf, id_buf,
    mine, pair_in, part, relay_in, direct_in, halo_out, halo_in, gather,
    field_sem, small_sem, barrier_send, barrier_recv,
    pair_send, pair_recv, ring_send, ring_recv, edge_send, edge_recv, out_send, out_recv,
):
    nka, ndev, rows, cols, taps = sizes
    del barrier_send, barrier_recv
    radius = (taps - 1) // 2
    nx = nka // 2
    width = cols // nka
    ext_rows = rows + 2 * radius
    half = rows // 2

    ka = lax.axis_index("ka")
    dev = lax.axis_index("dev")
    x, core = ka // 2, ka % 2
    xs = [lax.rem(x + step, nx) for step in (0, 1, 2, 3)]
    right, left, far = xs[1], xs[3], xs[2]
    to_right = (right * 2 + core, dev)
    to_left = (left * 2 + core, dev)
    to_sib = (x * 2 + 1 - core, dev)
    below = (ka, lax.rem(dev + ndev - 1, ndev))
    above = (ka, lax.rem(dev + 1, ndev))

    order = []
    for place in (far, right, left, x):
        order += [place * 2 + 1 - core, place * 2 + core]

    def columns(chunk):
        return pl.ds(pl.multiple_of(chunk * width, width), width)

    loads = []
    for k, chunk in enumerate(order):
        loads.append(
            (
                pltpu.make_async_copy(fwd.at[0, :, :, columns(chunk)], fwd_buf.at[k], field_sem.at[2 * k]),
                pltpu.make_async_copy(adj.at[0, :, :, columns(chunk)], adj_buf.at[k], field_sem.at[2 * k + 1]),
            )
        )
    block = pl.ds(pl.multiple_of((dev // 2) * 128, 128), 128)
    load_weights = pltpu.make_async_copy(weights, weight_buf, small_sem.at[0])
    load_ids = pltpu.make_async_copy(ids, id_buf, small_sem.at[1])
    load_band = pltpu.make_async_copy(band_t.at[:, block], band_buf, small_sem.at[2])
    load_density = pltpu.make_async_copy(density, ext.at[pl.ds(radius, rows)], small_sem.at[3])
    load_weights.start()
    load_ids.start()
    for pair in loads[:2]:
        for load in pair:
            load.start()
    load_band.start()
    for pair in loads[2:]:
        for load in pair:
            load.start()
    load_density.start()

    barrier = pltpu.get_barrier_semaphore()
    for target in (to_sib, to_right, to_left, below, above):
        pl.semaphore_signal(barrier, inc=1, device_id=target, device_id_type=MESH)
    pl.semaphore_wait(barrier, 5)

    started = []

    def send(src, dst, send_sem, recv_sem, target):
        copy = pltpu.make_async_remote_copy(
            src_ref=src, dst_ref=dst, send_sem=send_sem, recv_sem=recv_sem,
            device_id=target, device_id_type=MESH,
        )
        copy.start()
        started.append(copy)
        return copy

    dens_up = send(
        density.at[pl.ds(rows - radius, radius)], ext.at[pl.ds(0, radius)],
        edge_send.at[0], edge_recv.at[0], above,
    )
    dens_down = send(
        density.at[pl.ds(0, radius)], ext.at[pl.ds(rows + radius, radius)],
        edge_send.at[1], edge_recv.at[1], below,
    )

    load_weights.wait()
    load_ids.wait()
    weight = weight_buf[id_buf[ka]]

    def term(k):
        total = None
        for c in range(6):
            product = fwd_buf[k, c].astype(jnp.float32) * adj_buf[k, c].astype(jnp.float32)
            if total is None:
                total = product
            elif c < 3:
                total = total + product
            else:
                total = total - product
        return weight * total

    pairs = []
    for k in range(8):
        for load in loads[k]:
            load.wait()
        mine[k] = term(k)
        if k % 2 == 0:
            pairs.append(
                send(mine.at[k], pair_in.at[k // 2], pair_send.at[k // 2], pair_recv.at[k // 2], to_sib)
            )

    upper, lower = pl.ds(0, half), pl.ds(half, half)
    pairs[0].wait_recv()
    part[0] = mine[1] + pair_in[0]
    far_right = send(part.at[0, upper], relay_in.at[0], ring_send.at[0], ring_recv.at[0], to_right)
    far_left = send(part.at[0, lower], relay_in.at[1], ring_send.at[1], ring_recv.at[1], to_left)
    pairs[1].wait_recv()
    part[1] = mine[3] + pair_in[1]
    near_right = send(part.at[1, lower], direct_in.at[0, lower], ring_send.at[2], ring_recv.at[2], to_right)
    pairs[2].wait_recv()
    part[2] = mine[5] + pair_in[2]
    near_left = send(part.at[2, upper], direct_in.at[1, upper], ring_send.at[3], ring_recv.at[3], to_left)

    load_band.wait()
    band = band_buf[...]
    band = band / jnp.sum(band, axis=0, keepdims=True)
    band = jnp.concatenate([band, jnp.zeros((128 - taps, 128), jnp.float32)], axis=0)
    band_rows[...] = band.T
    taps_of = band_rows[pl.ds(pl.multiple_of(lax.rem(dev, 2) * rows, rows), rows), :]
    matrix = pltpu.roll(taps_of, 0, 1, stride=1, stride_axis=0)
    high, low = split(matrix)
    high32, low32 = high.astype(jnp.float32), low.astype(jnp.float32)
    stacked = jnp.concatenate([high32, high32, low32, jnp.zeros_like(high32)], axis=0)
    mat_t[...] = stacked.T.astype(jnp.bfloat16)
    mat[:, 0:128] = jnp.concatenate([high32[:, :ext_rows], high32[:, : 128 - ext_rows]], axis=1).astype(jnp.bfloat16)
    mat[:, 128:256] = jnp.concatenate(
        [
            high32[:, 128 - ext_rows : ext_rows],
            low32[:, :ext_rows],
            jnp.zeros((rows, 256 - 3 * ext_rows), jnp.float32),
        ],
        axis=1,
    ).astype(jnp.bfloat16)

    far_right.wait_recv()
    part[1, upper] = part[1, upper] + relay_in[0]
    sum_right = send(part.at[1, upper], direct_in.at[0, upper], ring_send.at[4], ring_recv.at[4], to_right)
    far_left.wait_recv()
    part[2, lower] = part[2, lower] + relay_in[1]
    sum_left = send(part.at[2, lower], direct_in.at[1, lower], ring_send.at[5], ring_recv.at[5], to_left)

    load_density.wait()
    dens_up.wait_recv()
    dens_down.wait_recv()
    first = jnp.where(dev == 0, 0.0, 1.0)
    last = jnp.where(dev == ndev - 1, 0.0, 1.0)
    quot = jnp.tanh(jnp.float32(BETA * ETA)) + jnp.tanh(jnp.float32(BETA * (1.0 - ETA)))
    shift = jnp.tanh(jnp.float32(BETA * ETA))
    ext[pl.ds(0, radius)] = ext[pl.ds(0, radius)] * first
    ext[pl.ds(rows + radius, radius)] = ext[pl.ds(rows + radius, radius)] * last
    for chunk in range(nka):
        at = slice(chunk * width, (chunk + 1) * width)
        high, low = split(ext[:, at])
        operand = jnp.concatenate(
            [high, low, high, jnp.zeros((256 - 3 * ext_rows, width), jnp.bfloat16)], axis=0
        )
        filtered = jnp.dot(mat[...], operand, preferred_element_type=jnp.float32)
        inner = jnp.tanh(BETA * (filtered - ETA))
        projected[:, at] = (shift + inner) / quot
        inner_buf[chunk] = inner
    inner = inner_buf[ka]
    slope = BETA * (1.0 - inner * inner) / quot

    pairs[3].wait_recv()
    sens = mine[7] + pair_in[3]
    near_right.wait_recv()
    near_left.wait_recv()
    sum_right.wait_recv()
    sum_left.wait_recv()
    sens = sens + direct_in[0] + direct_in[1]
    grad = 11.1 * slope * sens

    high, low = split(grad)
    operand = jnp.concatenate([high, low, high, jnp.zeros_like(high)], axis=0)
    spread = jnp.dot(mat_t[0:ext_rows, :], operand, preferred_element_type=jnp.float32)
    halo_out[0] = spread[0:radius]
    halo_out[1] = spread[rows + radius :]
    halo_down = send(halo_out.at[0], halo_in.at[1], edge_send.at[2], edge_recv.at[2], below)
    halo_up = send(halo_out.at[1], halo_in.at[0], edge_send.at[3], edge_recv.at[3], above)

    edge, inside = 2 * radius, rows - 2 * radius
    gather[ka, edge:rows] = spread[2 * radius : rows]
    parts = (
        (pl.ds(edge, inside), pl.ds(edge, inside // 2), pl.ds(edge + inside // 2, inside // 2)),
        (pl.ds(0, edge), pl.ds(0, edge // 2), pl.ds(edge // 2, edge // 2)),
    )

    def hand(chunk, rows_at, slot, target):
        return send(
            gather.at[chunk, rows_at], gather.at[chunk, rows_at], out_send.at[slot], out_recv.at[slot], target
        )

    def own(p, base):
        whole = parts[p][0]
        return (
            hand(ka, whole, base, to_right),
            hand(ka, whole, base + 1, to_left),
            hand(ka, whole, base + 2, to_sib),
        )

    first_out = own(0, 0)
    halo_up.wait_recv()
    halo_down.wait_recv()
    gather[ka, 0:radius] = spread[radius : 2 * radius] + halo_in[0] * first
    gather[ka, radius:edge] = spread[rows : rows + radius] + halo_in[1] * last
    second_out = own(1, 9)

    from_left, from_right, from_far = left * 2 + core, right * 2 + core, far * 2 + core
    relays = []
    for p, (outs, base) in enumerate(((first_out, 0), (second_out, 9))):
        whole, one, two = parts[p]
        outs[0].wait_recv()
        relay_right = hand(from_left, one, base + 3, to_right)
        sib_left = hand(from_left, whole, base + 5, to_sib)
        outs[1].wait_recv()
        relay_left = hand(from_right, two, base + 4, to_left)
        sib_right = hand(from_right, whole, base + 6, to_sib)
        relays.append((relay_right, relay_left, sib_left, sib_right))
    done = []
    for p, (relay, base) in enumerate(zip(relays, (0, 9))):
        whole, one, two = parts[p]
        relay[0].wait_recv()
        done.append(hand(from_far, one, base + 7, to_sib))
        relay[1].wait_recv()
        done.append(hand(from_far, two, base + 8, to_sib))

    def place(chunk):
        at = columns(chunk)
        design[0:radius, at] = gather[chunk, 0:radius]
        design[radius : rows - radius, at] = gather[chunk, edge:rows]
        design[rows - radius : rows, at] = gather[chunk, radius:edge]

    for chunk in (ka, from_left, from_right, from_far):
        place(chunk)
    first_out[2].wait_recv()
    second_out[2].wait_recv()
    place(x * 2 + 1 - core)
    for relay in relays:
        relay[2].wait_recv()
        relay[3].wait_recv()
    place(left * 2 + 1 - core)
    place(right * 2 + 1 - core)
    for copy in done:
        copy.wait_recv()
    place(far * 2 + 1 - core)

    for copy in started:
        copy.wait_send()


def solution(mesh):
    nka, ndev = mesh.shape["ka"], mesh.shape["dev"]

    def shards(density, fields_fwd, fields_adj, filter_band, k_weights, kpoint_ids):
        rows, cols = density.shape
        taps = filter_band.shape[1]
        radius = (taps - 1) // 2
        width = cols // nka
        ext_rows = rows + 2 * radius
        f32, bf16 = jnp.float32, jnp.bfloat16
        in_hbm = pl.BlockSpec(memory_space=pltpu.HBM)
        in_vmem = pl.BlockSpec(memory_space=pltpu.VMEM)
        dma = pltpu.SemaphoreType.DMA
        projected, design = pl.pallas_call(
            functools.partial(kernel, (nka, ndev, rows, cols, taps)),
            out_shape=[jax.ShapeDtypeStruct((rows, cols), f32)] * 2,
            in_specs=[in_hbm] * 6,
            out_specs=[in_vmem] * 2,
            scratch_shapes=[
                pltpu.VMEM((nka, 6, rows, width), bf16),
                pltpu.VMEM((nka, 6, rows, width), bf16),
                pltpu.VMEM((ext_rows, cols), f32),
                pltpu.VMEM((taps, 128), f32),
                pltpu.VMEM((128, 128), f32),
                pltpu.VMEM((rows, 256), bf16),
                pltpu.VMEM((128, 256), bf16),
                pltpu.VMEM((nka, rows, width), f32),
                pltpu.SMEM(k_weights.shape, f32),
                pltpu.SMEM(kpoint_ids.shape, jnp.int32),
                pltpu.VMEM((8, rows, width), f32),
                pltpu.VMEM((4, rows, width), f32),
                pltpu.VMEM((3, rows, width), f32),
                pltpu.VMEM((2, rows // 2, width), f32),
                pltpu.VMEM((2, rows, width), f32),
                pltpu.VMEM((2, radius, width), f32),
                pltpu.VMEM((2, radius, width), f32),
                pltpu.VMEM((nka, rows, width), f32),
                dma((16,)),
                dma((4,)),
                dma((1,)),
                dma((1,)),
                dma((4,)),
                dma((4,)),
                dma((6,)),
                dma((6,)),
                dma((4,)),
                dma((4,)),
                dma((18,)),
                dma((18,)),
            ],
            compiler_params=pltpu.CompilerParams(
                collective_id=0, has_side_effects=True, vmem_limit_bytes=40 * 1024 * 1024
            ),
            name="sensitivities",
        )(
            *(
                pltpu.with_memory_space_constraint(operand, pltpu.HBM)
                for operand in (density, fields_fwd, fields_adj, filter_band.T, k_weights, kpoint_ids)
            )
        )
        return projected, design

    return jax.shard_map(
        shards,
        mesh=mesh,
        in_specs=(
            P("dev", None),
            P("ka", None, "dev", None),
            P("ka", None, "dev", None),
            P(),
            P(),
            P(),
        ),
        out_specs=(P("dev", None), P("dev", None)),
        check_vma=False,
    )
```

```python
import functools

import jax
import jax.numpy as jnp
from jax import lax
from jax.experimental import pallas as pl
from jax.experimental.pallas import tpu as pltpu
from jax.sharding import PartitionSpec as P

MESH = pl.DeviceIdType.MESH
BETA, ETA = 8.0, 0.5
F32, BF16 = jnp.float32, jnp.bfloat16


def split(value):
    high = value.astype(BF16)
    low = (value - high.astype(F32)).astype(BF16)
    return high, low


def kernel(
    sizes,
    density, fwd, adj, band_t, weights, ids,
    projected, design,
    fields, terms, pair_in, part, sum_in, edge_in,
    ext, dens_cols, band_buf, band_rows, mat, mat_wide, mat_t, mat_edge, weight_buf, id_buf, inner_rows, end_rows,
    load_sem, small_sem, ready, pair_send, pair_recv, sum_send, sum_recv,
    dens_send, dens_recv, edge_send, edge_recv, out_send, out_recv,
):
    nka, ndev, rows, cols, taps = sizes
    radius = (taps - 1) // 2
    nx = nka // 2
    half = cols // 2
    width = half // nka
    ext_rows = rows + 2 * radius
    side = 2 * radius

    ka = lax.axis_index("ka")
    dev = lax.axis_index("dev")
    x, core = ka // 2, lax.rem(ka, 2)
    mine = core * nx + x
    xs = [lax.rem(x + step, nx) for step in range(nx)]
    sib = (x * 2 + 1 - core, dev)
    line = [(xs[step] * 2 + core, dev) for step in range(nx)]
    dev_up, dev_down = lax.rem(dev + 1, ndev), lax.rem(dev + ndev - 1, ndev)
    up = [(xs[step] * 2 + core, dev_up) for step in range(nx)]
    down = [(xs[step] * 2 + core, dev_down) for step in range(nx)]
    has_up, has_down = dev < ndev - 1, dev > 0
    even_up, even_down = has_up & (lax.rem(dev, 16) == 15), has_down & (lax.rem(dev, 16) == 0)
    early_up = has_up & (lax.rem(dev, 4) != 3)
    early_down = has_down & (lax.rem(dev, 4) == 0) & (lax.rem(dev, 16) != 0)
    late_up, late_down = has_up & ~early_up, has_down & ~early_down

    def columns(h, chunk):
        return pl.ds(pl.multiple_of(h * half + chunk * width, width), width)

    def load(src, dst, sem):
        copy = pltpu.make_async_copy(src, dst, sem)
        copy.start()
        return copy

    def arrived(ref, sem):
        pltpu.make_async_copy(ref, ref, sem).wait()

    def chunks(h, which):
        return pl.ds(pl.multiple_of(h * half + which * nx * width, nx * width), nx * width)

    def load_chunks(h, which, sem):
        at = chunks(h, which)
        load(fwd.at[0, :, :, at], fields.at[0, :, :, at], load_sem.at[sem])
        load(adj.at[0, :, :, at], fields.at[1, :, :, at], load_sem.at[sem])

    small = [
        load(weights, weight_buf, small_sem.at[0]),
        load(ids, id_buf, small_sem.at[1]),
    ]
    load_chunks(0, 1 - core, 0)
    load_chunks(0, core, 1)
    first_band = lax.max(dev * rows - radius, 0) // 128
    last_band = lax.min((dev * rows - radius + 128) // 128, (ndev * rows - 1) // 128)
    for n, block in enumerate((first_band, last_band)):
        load(band_t.at[:, pl.ds(pl.multiple_of(block * 128, 128), 128)], band_buf.at[n], small_sem.at[2])
    load_chunks(1, 1 - core, 2)
    load_chunks(1, core, 3)
    own_rows = pl.ds(side, rows)
    for h in range(2):
        load(density.at[:, columns(h, mine)], dens_cols.at[h, own_rows], small_sem.at[3])
    load_density = load(density, ext.at[pl.ds(radius, rows)], small_sem.at[4])

    barrier = pltpu.get_barrier_semaphore()

    def greet(semaphore, targets):
        for target in targets:
            pl.semaphore_signal(semaphore, inc=1, device_id=target, device_id_type=MESH)

    greet(barrier, [sib] + line[1:])

    @pl.when(early_up | even_up)
    def _():
        greet(barrier, up)

    @pl.when(early_down | even_down)
    def _():
        greet(barrier, down)

    def remote(src, dst, send_sem, recv_sem, target):
        return pltpu.make_async_remote_copy(
            src_ref=src, dst_ref=dst, send_sem=send_sem, recv_sem=recv_sem,
            device_id=target, device_id_type=MESH,
        )

    @pl.when(dev == 0)
    def _():
        ext[pl.ds(0, radius)] = jnp.zeros((radius, cols), F32)
        dens_cols[:, pl.ds(0, side)] = jnp.zeros((2, side, width), F32)
        edge_in[0] = jnp.zeros((nx, 2, radius, width), F32)

    @pl.when(dev == ndev - 1)
    def _():
        ext[pl.ds(radius + rows, radius)] = jnp.zeros((radius, cols), F32)
        dens_cols[:, pl.ds(side + rows, side)] = jnp.zeros((2, side, width), F32)
        edge_in[1] = jnp.zeros((nx, 2, radius, width), F32)

    for copy in small:
        copy.wait()
    weight = weight_buf[id_buf[ka]]

    def fill_terms(h, which, sem):
        arrived(fields.at[:, :, :, chunks(h, which)], load_sem.at[sem])
        for quarter in range(nx):
            at = columns(h, which * nx + quarter)
            total = None
            for c in range(6):
                product = fields[0, c, :, at].astype(F32) * fields[1, c, :, at].astype(F32)
                total = product if total is None else total + product if c < 3 else total - product
            terms[h, which, quarter] = weight * total

    pairs = [
        [
            remote(
                terms.at[h, 1 - core, xs[step]], pair_in.at[h, xs[step]],
                pair_send.at[0], pair_recv.at[h * nx + n], sib,
            )
            for n, step in enumerate((2, 1, 3, 0))
        ]
        for h in range(2)
    ]
    fill_terms(0, 1 - core, 0)

    one = jnp.int32(1)
    greeted = nx + nx * (jnp.where(late_down, one, 0) + jnp.where(late_up, one, 0))
    pl.semaphore_wait(barrier, greeted)

    @pl.when(late_down & ~even_down)
    def _():
        greet(ready.at[0], down)

    @pl.when(late_up & ~even_up)
    def _():
        greet(ready.at[1], up)

    for copy in pairs[0]:
        copy.start()

    first_side, last_side = pl.ds(0, side), pl.ds(rows - side, side)
    cols_down = [
        remote(
            density.at[first_side, columns(h, mine)], dens_cols.at[h, pl.ds(side + rows, side)],
            dens_send.at[0], dens_recv.at[0], down[0],
        )
        for h in range(2)
    ]
    cols_up = [
        remote(
            density.at[last_side, columns(h, mine)], dens_cols.at[h, first_side],
            dens_send.at[1], dens_recv.at[1], up[0],
        )
        for h in range(2)
    ]
    rows_down = remote(
        density.at[pl.ds(0, radius)], ext.at[pl.ds(radius + rows, radius)], dens_send.at[2], dens_recv.at[2], down[0]
    )
    rows_up = remote(
        density.at[pl.ds(rows - radius, radius)], ext.at[pl.ds(0, radius)], dens_send.at[3], dens_recv.at[3], up[0]
    )

    edges_down = [
        remote(part.at[:, xs[s], pl.ds(0, radius)], edge_in.at[1, s], edge_send.at[0], edge_recv.at[0], down[s])
        for s in range(nx)
    ]
    edges_up = [
        remote(
            part.at[:, xs[s], pl.ds(rows - radius, radius)], edge_in.at[0, s],
            edge_send.at[1], edge_recv.at[1], up[s],
        )
        for s in range(nx)
    ]

    @pl.when(late_down)
    def _():
        for copy in cols_down:
            copy.start()

    @pl.when(late_up)
    def _():
        for copy in cols_up:
            copy.start()

    fill_terms(0, core, 1)
    fill_terms(1, 1 - core, 2)
    for copy in pairs[1]:
        copy.start()
    for h in range(2):
        if h == 1:
            fill_terms(1, core, 3)
        for n, step in enumerate((2, 1, 3, 0)):
            pairs[h][n].wait_recv()
            part[h, xs[step]] = terms[h, core, xs[step]] + pair_in[h, xs[step]]
            if step:
                remote(
                    part.at[h, xs[step]], sum_in.at[h, step - 1], sum_send.at[0], sum_recv.at[h], line[step]
                ).start()
        if h == 1:

            @pl.when(late_down)
            def _():
                for copy in edges_down:
                    copy.start()

            @pl.when(late_up)
            def _():
                for copy in edges_up:
                    copy.start()

    @pl.when(late_down)
    def _():
        rows_down.start()

    @pl.when(late_up)
    def _():
        rows_up.start()

    arrived(band_buf, small_sem.at[2])
    for n in range(2):
        band = band_buf[n]
        band = band / jnp.sum(band, axis=0, keepdims=True)
        band = jnp.concatenate([band, jnp.zeros((128 - taps, 128), F32)], axis=0)
        band_rows[n * 128 : (n + 1) * 128] = band.T
    offset = jnp.where(lax.rem(dev, 2) == 0, 128 - radius, rows - radius)
    band_ext = band_rows[pl.ds(pl.multiple_of(offset, radius), ext_rows), :]

    def shear(value, shift):
        return pltpu.roll(value, shift, 1, stride=1, stride_axis=0)

    def parts_of(value):
        high, low = split(value)
        return high.astype(F32), low.astype(F32)

    high, low = parts_of(shear(band_ext, 0))
    mat_wide[:, 0:128] = high.astype(BF16)
    mat_wide[:, 128:256] = high.astype(BF16)
    mat_wide[:, 256:384] = low.astype(BF16)
    high, low = parts_of(shear(band_ext, 128 - 2 * radius))
    stacked = jnp.concatenate([high, high, low, jnp.zeros((256 - 3 * ext_rows, 128), F32)], axis=0).T
    mat_t[...] = stacked[0:rows].astype(BF16)
    mat_edge[...] = jnp.concatenate([stacked[0:radius], stacked[rows - radius : rows]], axis=0).astype(BF16)
    high, low = parts_of(shear(band_ext[radius : radius + rows], 0))
    mat[:, 0:128] = jnp.concatenate([high[:, :ext_rows], high[:, : 128 - ext_rows]], axis=1).astype(BF16)
    mat[:, 128:256] = jnp.concatenate(
        [high[:, 128 - ext_rows : ext_rows], low[:, :ext_rows], jnp.zeros((rows, 256 - 3 * ext_rows), F32)], axis=1
    ).astype(BF16)

    @pl.when(early_up)
    def _():
        pl.semaphore_wait(ready.at[0], nx)
        for copy in cols_up + edges_up + [rows_up]:
            copy.start()

    @pl.when(early_down)
    def _():
        pl.semaphore_wait(ready.at[1], nx)
        for copy in cols_down + edges_down + [rows_down]:
            copy.start()

    quot = jnp.tanh(jnp.float32(BETA * ETA)) + jnp.tanh(jnp.float32(BETA * (1.0 - ETA)))
    shift = jnp.tanh(jnp.float32(BETA * ETA))
    arrived(dens_cols.at[:, own_rows], small_sem.at[3])
    upper_side = pl.ds(side + rows, side)

    @pl.when(has_down)
    def _():
        arrived(dens_cols.at[:, first_side], dens_recv.at[1])

    @pl.when(has_up)
    def _():
        arrived(dens_cols.at[:, upper_side], dens_recv.at[0])

    high, low = split(jnp.concatenate([dens_cols[0], dens_cols[1]], axis=1))
    gap = jnp.zeros((128 - ext_rows - 2 * radius, 2 * width), BF16)
    operand = jnp.concatenate([high, gap, low, gap, high, gap], axis=0)
    filtered = jnp.dot(mat_wide[...], operand, preferred_element_type=F32)
    inner = jnp.tanh(BETA * (filtered - ETA))
    slope = 11.1 * BETA * (1.0 - inner * inner) / quot

    def transposed(matrix, value):
        high, low = split(value)
        pad = jnp.zeros((256 - 3 * ext_rows, value.shape[1]), BF16)
        return jnp.dot(matrix, jnp.concatenate([high, low, high, pad], axis=0), preferred_element_type=F32)

    def hand(buffer, slot, target):
        remote(buffer, buffer, out_send.at[slot // 2], out_recv.at[slot], target).start()

    chip = pl.ds(core * nx, nx)
    three = pl.ds(0, nx - 1)
    none = jnp.zeros((radius, width), F32)
    grads = []
    for h in range(2):
        arrived(sum_in.at[h], sum_recv.at[h])
        sens = (part[h, x] + sum_in[h, 0]) + (sum_in[h, 1] + sum_in[h, 2])
        grads.append(slope[radius : radius + rows, h * width : (h + 1) * width] * sens)
        own = transposed(mat_t[...], jnp.concatenate([none, grads[h], none], axis=0))
        inner_rows[h, mine] = own[radius : rows - radius]
        for step in (2, 1, 3):
            hand(inner_rows.at[h, mine], h, line[step])

    @pl.when(has_up)
    def _():
        arrived(edge_in.at[1], edge_recv.at[0])

    @pl.when(has_down)
    def _():
        arrived(edge_in.at[0], edge_recv.at[1])

    edge = edge_in[:, 0] + edge_in[:, 1] + (edge_in[:, 2] + edge_in[:, 3])
    first, last = [jnp.concatenate([edge[n, 0], edge[n, 1]], axis=1) for n in range(2)]
    grad = jnp.concatenate(
        [slope[0:radius] * first, jnp.concatenate(grads, axis=1), slope[radius + rows :] * last], axis=0
    )
    ends = transposed(mat_edge[...], grad)
    for h in range(2):
        end_rows[mine, h] = ends[:, h * width : (h + 1) * width]
    for step in (2, 1, 3):
        hand(end_rows.at[mine], 4, line[step])

    load_density.wait()

    @pl.when(has_down)
    def _():
        rows_up.wait_recv()

    @pl.when(has_up)
    def _():
        rows_down.wait_recv()

    for chunk in range(8):
        at = slice(chunk * cols // 8, (chunk + 1) * cols // 8)
        high, low = split(ext[:, at])
        pad = jnp.zeros((256 - 3 * ext_rows, cols // 8), BF16)
        operand = jnp.concatenate([high, low, high, pad], axis=0)
        filtered = jnp.dot(mat[...], operand, preferred_element_type=F32)
        projected[:, at] = (shift + jnp.tanh(BETA * (filtered - ETA))) / quot

    for h in range(2):
        arrived(inner_rows.at[h, three], out_recv.at[h])
        hand(inner_rows.at[h, chip], 2 + h, sib)
    arrived(end_rows.at[three], out_recv.at[4])
    hand(end_rows.at[chip], 6, sib)

    def place_inner(h, which):
        for quarter in range(nx):
            chunk = which * nx + quarter
            design[radius : rows - radius, columns(h, chunk)] = inner_rows[h, chunk]

    def place_ends(which):
        for quarter in range(nx):
            chunk = which * nx + quarter
            for h in range(2):
                design[0:radius, columns(h, chunk)] = end_rows[chunk, h, 0:radius]
                design[rows - radius : rows, columns(h, chunk)] = end_rows[chunk, h, radius:side]

    for h in range(2):
        place_inner(h, core)
    place_ends(core)
    other = pl.ds((1 - core) * nx, nx)
    for h in range(2):
        arrived(inner_rows.at[h, other], out_recv.at[2 + h])
        place_inner(h, 1 - core)
    arrived(end_rows.at[other], out_recv.at[6])
    place_ends(1 - core)

    arrived(pair_in, pair_send.at[0])
    arrived(sum_in, sum_send.at[0])
    arrived(inner_rows.at[:, three], out_send.at[0])
    arrived(inner_rows.at[:, chip], out_send.at[1])
    arrived(end_rows.at[three], out_send.at[2])
    arrived(end_rows.at[chip], out_send.at[3])

    @pl.when(has_down)
    def _():
        arrived(dens_cols.at[:, first_side], dens_send.at[0])
        rows_down.wait_send()
        arrived(edge_in.at[1], edge_send.at[0])

    @pl.when(has_up)
    def _():
        arrived(dens_cols.at[:, first_side], dens_send.at[1])
        rows_up.wait_send()
        arrived(edge_in.at[0], edge_send.at[1])


def write(projected, design, projected_out, design_out, sem):
    copies = [
        pltpu.make_async_copy(projected, projected_out, sem.at[0]),
        pltpu.make_async_copy(design, design_out, sem.at[1]),
    ]
    for copy in copies:
        copy.start()
    for copy in copies:
        copy.wait()


def solution(mesh):
    nka, ndev = mesh.shape["ka"], mesh.shape["dev"]

    def shards(density, fields_fwd, fields_adj, filter_band, k_weights, kpoint_ids):
        rows, cols = density.shape
        taps = filter_band.shape[1]
        radius = (taps - 1) // 2
        nx, width = nka // 2, cols // 2 // nka
        ext_rows = rows + 2 * radius
        in_vmem = pl.BlockSpec(memory_space=pltpu.VMEM)
        dma = pltpu.SemaphoreType.DMA
        results = pl.pallas_call(
            functools.partial(kernel, (nka, ndev, rows, cols, taps)),
            out_shape=[jax.ShapeDtypeStruct((rows, cols), F32)] * 2,
            in_specs=[pl.BlockSpec(memory_space=pltpu.HBM)] * 6,
            out_specs=[in_vmem] * 2,
            scratch_shapes=[
                pltpu.VMEM((2, 6, rows, cols), BF16),
                pltpu.VMEM((2, 2, nx, rows, width), F32),
                pltpu.VMEM((2, nx, rows, width), F32),
                pltpu.VMEM((2, nx, rows, width), F32),
                pltpu.VMEM((2, nx - 1, rows, width), F32),
                pltpu.VMEM((2, nx, 2, radius, width), F32),
                pltpu.VMEM((ext_rows, cols), F32),
                pltpu.VMEM((2, ext_rows + 2 * radius, width), F32),
                pltpu.VMEM((2, taps, 128), F32),
                pltpu.VMEM((256, 128), F32),
                pltpu.VMEM((rows, 256), BF16),
                pltpu.VMEM((ext_rows, 384), BF16),
                pltpu.VMEM((rows, 256), BF16),
                pltpu.VMEM((2 * radius, 256), BF16),
                pltpu.SMEM(k_weights.shape, F32),
                pltpu.SMEM(kpoint_ids.shape, jnp.int32),
                pltpu.VMEM((2, nka, rows - 2 * radius, width), F32),
                pltpu.VMEM((nka, 2, 2 * radius, width), F32),
                dma((4,)),
                dma((5,)),
                pltpu.SemaphoreType.REGULAR((2,)),
                dma((1,)),
                dma((2 * nx,)),
                dma((1,)),
                dma((2,)),
                dma((4,)),
                dma((4,)),
                dma((2,)),
                dma((2,)),
                dma((4,)),
                dma((7,)),
            ],
            compiler_params=pltpu.CompilerParams(
                collective_id=0, has_side_effects=True, vmem_limit_bytes=40 * 1024 * 1024
            ),
            name="sensitivities",
        )(
            *(
                pltpu.with_memory_space_constraint(operand, pltpu.HBM)
                for operand in (density, fields_fwd, fields_adj, filter_band.T, k_weights, kpoint_ids)
            )
        )
        return pl.pallas_call(
            write,
            out_shape=[jax.ShapeDtypeStruct((rows, cols), F32)] * 2,
            in_specs=[in_vmem] * 2,
            out_specs=[pl.BlockSpec(memory_space=pltpu.HBM)] * 2,
            scratch_shapes=[dma((2,))],
            name="write_results",
        )(*(pltpu.with_memory_space_constraint(result, pltpu.VMEM) for result in results))

    return jax.shard_map(
        shards,
        mesh=mesh,
        in_specs=(
            P("dev", None),
            P("ka", None, "dev", None),
            P("ka", None, "dev", None),
            P(),
            P(),
            P(),
        ),
        out_specs=(P("dev", None), P("dev", None)),
        check_vma=False,
    )
```

```python
import functools

import jax
import jax.numpy as jnp
from jax import lax
from jax.experimental import pallas as pl
from jax.experimental.pallas import tpu as pltpu
from jax.sharding import PartitionSpec as P

MESH = pl.DeviceIdType.MESH
BETA, ETA = 8.0, 0.5
F32, BF16 = jnp.float32, jnp.bfloat16


def split(value):
    high = value.astype(BF16)
    low = (value - high.astype(F32)).astype(BF16)
    return high, low


def kernel(
    sizes,
    density, fwd, adj, band_t, weights, ids,
    projected, design,
    fields, terms, pair_in, part, sum_in, edge_in,
    ext, dens_cols, band_buf, band_rows, mat, mat_wide, mat_t, mat_edge, weight_buf, id_buf, inner_rows, end_rows,
    load_sem, small_sem, ready, pair_send, pair_recv, sum_send, sum_recv,
    dens_send, dens_recv, edge_send, edge_recv, out_send, out_recv,
):
    nka, ndev, rows, cols, taps = sizes
    radius = (taps - 1) // 2
    nx = nka // 2
    half = cols // 2
    width = half // nka
    ext_rows = rows + 2 * radius
    side = 2 * radius

    ka = lax.axis_index("ka")
    dev = lax.axis_index("dev")
    x, core = ka // 2, lax.rem(ka, 2)
    mine = core * nx + x
    xs = [lax.rem(x + step, nx) for step in range(nx)]
    sib = (x * 2 + 1 - core, dev)
    line = [(xs[step] * 2 + core, dev) for step in range(nx)]
    dev_up, dev_down = lax.rem(dev + 1, ndev), lax.rem(dev + ndev - 1, ndev)
    up = [(xs[step] * 2 + core, dev_up) for step in range(nx)]
    down = [(xs[step] * 2 + core, dev_down) for step in range(nx)]
    has_up, has_down = dev < ndev - 1, dev > 0
    even_up, even_down = has_up & ((dev == 15) | (dev == 31)), has_down & ((dev == 16) | (dev == 32))
    early_up = has_up & (lax.rem(dev, 4) != 3) & (dev != 0)
    early_down = has_down & ((lax.rem(dev, 4) == 0) | (dev == 1)) & ~even_down
    late_up, late_down = has_up & ~early_up, has_down & ~early_down
    late_chip = jnp.where(dev == 0, 0, nx // 2)
    is_late = x == late_chip

    def columns(h, chunk):
        return pl.ds(pl.multiple_of(h * half + chunk * width, width), width)

    def load(src, dst, sem):
        copy = pltpu.make_async_copy(src, dst, sem)
        copy.start()
        return copy

    def arrived(ref, sem):
        pltpu.make_async_copy(ref, ref, sem).wait()

    def chunks(h, which):
        return pl.ds(pl.multiple_of(h * half + which * nx * width, nx * width), nx * width)

    def load_chunks(h, which, sem):
        at = chunks(h, which)
        load(fwd.at[0, :, :, at], fields.at[0, :, :, at], load_sem.at[sem])
        load(adj.at[0, :, :, at], fields.at[1, :, :, at], load_sem.at[sem])

    small = [
        load(weights, weight_buf, small_sem.at[0]),
        load(ids, id_buf, small_sem.at[1]),
    ]
    load_chunks(0, 1 - core, 0)
    load_chunks(0, core, 1)
    load_chunks(1, 1 - core, 2)
    load_chunks(1, core, 3)

    barrier = pltpu.get_barrier_semaphore()

    def greet(semaphore, targets):
        for target in targets:
            pl.semaphore_signal(semaphore, inc=1, device_id=target, device_id_type=MESH)

    greet(barrier, [sib])

    @pl.when(~is_late)
    def _():
        greet(barrier, line[1:])

    @pl.when(early_up | even_up)
    def _():
        greet(barrier, up)

    @pl.when(early_down | even_down)
    def _():
        greet(barrier, down)

    one = jnp.int32(1)
    greeted = nx - 1 + jnp.where(is_late, one, 0) + nx * (jnp.where(late_down, one, 0) + jnp.where(late_up, one, 0))

    def answer():
        @pl.when(late_down & ~even_down)
        def _():
            greet(ready.at[0], down)

        @pl.when(late_up & ~even_up)
        def _():
            greet(ready.at[1], up)

    @pl.when(is_late)
    def _():
        pl.semaphore_wait(barrier, greeted)
        greet(ready.at[2], line[1:])
        answer()

    first_band = lax.max(dev * rows - radius, 0) // 128
    last_band = lax.min((dev * rows - radius + 128) // 128, (ndev * rows - 1) // 128)
    for n, block in enumerate((first_band, last_band)):
        load(band_t.at[:, pl.ds(pl.multiple_of(block * 128, 128), 128)], band_buf.at[n], small_sem.at[2])
    own_rows = pl.ds(side, rows)
    for h in range(2):
        load(density.at[:, columns(h, mine)], dens_cols.at[h, own_rows], small_sem.at[3])
    load_density = load(density, ext.at[pl.ds(radius, rows)], small_sem.at[4])

    def remote(src, dst, send_sem, recv_sem, target):
        return pltpu.make_async_remote_copy(
            src_ref=src, dst_ref=dst, send_sem=send_sem, recv_sem=recv_sem,
            device_id=target, device_id_type=MESH,
        )

    @pl.when(dev == 0)
    def _():
        ext[pl.ds(0, radius)] = jnp.zeros((radius, cols), F32)
        dens_cols[:, pl.ds(0, side)] = jnp.zeros((2, side, width), F32)
        edge_in[0] = jnp.zeros((nx, 2, radius, width), F32)

    @pl.when(dev == ndev - 1)
    def _():
        ext[pl.ds(radius + rows, radius)] = jnp.zeros((radius, cols), F32)
        dens_cols[:, pl.ds(side + rows, side)] = jnp.zeros((2, side, width), F32)
        edge_in[1] = jnp.zeros((nx, 2, radius, width), F32)

    for copy in small:
        copy.wait()
    weight = weight_buf[id_buf[ka]]

    def fill_terms(h, which, sem):
        arrived(fields.at[:, :, :, chunks(h, which)], load_sem.at[sem])
        for quarter in range(nx):
            at = columns(h, which * nx + quarter)
            total = None
            for c in range(6):
                product = fields[0, c, :, at].astype(F32) * fields[1, c, :, at].astype(F32)
                total = product if total is None else total + product if c < 3 else total - product
            terms[h, which, quarter] = weight * total

    pairs = [remote(terms.at[h, 1 - core], pair_in.at[h], pair_send.at[0], pair_recv.at[h], sib) for h in range(2)]
    fill_terms(0, 1 - core, 0)

    @pl.when(~is_late)
    def _():
        pl.semaphore_wait(barrier, greeted)
        answer()

    pairs[0].start()

    first_side, last_side = pl.ds(0, side), pl.ds(rows - side, side)
    cols_down = [
        remote(
            density.at[first_side, columns(h, mine)], dens_cols.at[h, pl.ds(side + rows, side)],
            dens_send.at[0], dens_recv.at[0], down[0],
        )
        for h in range(2)
    ]
    cols_up = [
        remote(
            density.at[last_side, columns(h, mine)], dens_cols.at[h, first_side],
            dens_send.at[1], dens_recv.at[1], up[0],
        )
        for h in range(2)
    ]
    rows_down = remote(
        density.at[pl.ds(0, radius)], ext.at[pl.ds(radius + rows, radius)], dens_send.at[2], dens_recv.at[2], down[0]
    )
    rows_up = remote(
        density.at[pl.ds(rows - radius, radius)], ext.at[pl.ds(0, radius)], dens_send.at[3], dens_recv.at[3], up[0]
    )

    edges_down = [
        remote(part.at[:, xs[s], pl.ds(0, radius)], edge_in.at[1, s], edge_send.at[0], edge_recv.at[0], down[s])
        for s in range(nx)
    ]
    edges_up = [
        remote(
            part.at[:, xs[s], pl.ds(rows - radius, radius)], edge_in.at[0, s],
            edge_send.at[1], edge_recv.at[1], up[s],
        )
        for s in range(nx)
    ]

    @pl.when(late_down)
    def _():
        for copy in cols_down:
            copy.start()

    @pl.when(late_up)
    def _():
        for copy in cols_up:
            copy.start()

    fill_terms(0, core, 1)
    fill_terms(1, 1 - core, 2)
    pairs[1].start()
    for h in range(2):
        if h == 1:
            fill_terms(1, core, 3)
        pairs[h].wait_recv()
        for step in (2, 1, 3, 0):
            part[h, xs[step]] = terms[h, core, xs[step]] + pair_in[h, xs[step]]
            if step:
                copy = remote(
                    part.at[h, xs[step]], sum_in.at[h, step - 1], sum_send.at[0], sum_recv.at[h], line[step]
                )
                pl.when(is_late | (xs[step] != late_chip))(copy.start)
        if h == 1:

            @pl.when(late_down)
            def _():
                for copy in edges_down:
                    copy.start()

            @pl.when(late_up)
            def _():
                for copy in edges_up:
                    copy.start()

    @pl.when(~is_late)
    def _():
        pl.semaphore_wait(ready.at[2], 1)
        slot = lax.rem(late_chip - x + nx, nx) - 1
        for h in range(2):
            remote(
                part.at[h, late_chip], sum_in.at[h, slot], sum_send.at[0], sum_recv.at[h], (late_chip * 2 + core, dev)
            ).start()

    @pl.when(late_down)
    def _():
        rows_down.start()

    @pl.when(late_up)
    def _():
        rows_up.start()

    arrived(band_buf, small_sem.at[2])
    for n in range(2):
        band = band_buf[n]
        band = band / jnp.sum(band, axis=0, keepdims=True)
        band = jnp.concatenate([band, jnp.zeros((128 - taps, 128), F32)], axis=0)
        band_rows[n * 128 : (n + 1) * 128] = band.T
    offset = jnp.where(lax.rem(dev, 2) == 0, 128 - radius, rows - radius)
    band_ext = band_rows[pl.ds(pl.multiple_of(offset, radius), ext_rows), :]

    def shear(value, shift):
        return pltpu.roll(value, shift, 1, stride=1, stride_axis=0)

    def parts_of(value):
        high, low = split(value)
        return high.astype(F32), low.astype(F32)

    high, low = parts_of(shear(band_ext, 0))
    mat_wide[:, 0:128] = high.astype(BF16)
    mat_wide[:, 128:256] = high.astype(BF16)
    mat_wide[:, 256:384] = low.astype(BF16)
    high, low = parts_of(shear(band_ext, 128 - 2 * radius))
    stacked = jnp.concatenate([high, high, low, jnp.zeros((256 - 3 * ext_rows, 128), F32)], axis=0).T
    mat_t[...] = stacked[0:rows].astype(BF16)
    mat_edge[...] = jnp.concatenate([stacked[0:radius], stacked[rows - radius : rows]], axis=0).astype(BF16)
    high, low = parts_of(shear(band_ext[radius : radius + rows], 0))
    mat[:, 0:128] = jnp.concatenate([high[:, :ext_rows], high[:, : 128 - ext_rows]], axis=1).astype(BF16)
    mat[:, 128:256] = jnp.concatenate(
        [high[:, 128 - ext_rows : ext_rows], low[:, :ext_rows], jnp.zeros((rows, 256 - 3 * ext_rows), F32)], axis=1
    ).astype(BF16)

    @pl.when(early_up)
    def _():
        pl.semaphore_wait(ready.at[0], nx)
        for copy in cols_up + edges_up + [rows_up]:
            copy.start()

    @pl.when(early_down)
    def _():
        pl.semaphore_wait(ready.at[1], nx)
        for copy in cols_down + edges_down + [rows_down]:
            copy.start()

    quot = jnp.tanh(jnp.float32(BETA * ETA)) + jnp.tanh(jnp.float32(BETA * (1.0 - ETA)))
    shift = jnp.tanh(jnp.float32(BETA * ETA))
    arrived(dens_cols.at[:, own_rows], small_sem.at[3])
    upper_side = pl.ds(side + rows, side)

    @pl.when(has_down)
    def _():
        arrived(dens_cols.at[:, first_side], dens_recv.at[1])

    @pl.when(has_up)
    def _():
        arrived(dens_cols.at[:, upper_side], dens_recv.at[0])

    high, low = split(jnp.concatenate([dens_cols[0], dens_cols[1]], axis=1))
    gap = jnp.zeros((128 - ext_rows - 2 * radius, 2 * width), BF16)
    operand = jnp.concatenate([high, gap, low, gap, high, gap], axis=0)
    filtered = jnp.dot(mat_wide[...], operand, preferred_element_type=F32)
    inner = jnp.tanh(BETA * (filtered - ETA))
    slope = 11.1 * BETA * (1.0 - inner * inner) / quot

    def transposed(matrix, value):
        high, low = split(value)
        pad = jnp.zeros((256 - 3 * ext_rows, value.shape[1]), BF16)
        return jnp.dot(matrix, jnp.concatenate([high, low, high, pad], axis=0), preferred_element_type=F32)

    def hand(buffer, slot, target):
        remote(buffer, buffer, out_send.at[slot // 2], out_recv.at[slot], target).start()

    chip = pl.ds(core * nx, nx)
    three = pl.ds(0, nx - 1)
    none = jnp.zeros((radius, width), F32)
    grads = []
    for h in range(2):
        arrived(sum_in.at[h], sum_recv.at[h])
        sens = (part[h, x] + sum_in[h, 0]) + (sum_in[h, 1] + sum_in[h, 2])
        grads.append(slope[radius : radius + rows, h * width : (h + 1) * width] * sens)
        own = transposed(mat_t[...], jnp.concatenate([none, grads[h], none], axis=0))
        inner_rows[h, mine] = own[radius : rows - radius]
        for step in (2, 1, 3):
            hand(inner_rows.at[h, mine], h, line[step])

    @pl.when(has_up)
    def _():
        arrived(edge_in.at[1], edge_recv.at[0])

    @pl.when(has_down)
    def _():
        arrived(edge_in.at[0], edge_recv.at[1])

    edge = edge_in[:, 0] + edge_in[:, 1] + (edge_in[:, 2] + edge_in[:, 3])
    first, last = [jnp.concatenate([edge[n, 0], edge[n, 1]], axis=1) for n in range(2)]
    grad = jnp.concatenate(
        [slope[0:radius] * first, jnp.concatenate(grads, axis=1), slope[radius + rows :] * last], axis=0
    )
    ends = transposed(mat_edge[...], grad)
    for h in range(2):
        end_rows[mine, h] = ends[:, h * width : (h + 1) * width]
    for step in (2, 1, 3):
        hand(end_rows.at[mine], 4, line[step])

    load_density.wait()

    @pl.when(has_down)
    def _():
        rows_up.wait_recv()

    @pl.when(has_up)
    def _():
        rows_down.wait_recv()

    for chunk in range(8):
        at = slice(chunk * cols // 8, (chunk + 1) * cols // 8)
        high, low = split(ext[:, at])
        pad = jnp.zeros((256 - 3 * ext_rows, cols // 8), BF16)
        operand = jnp.concatenate([high, low, high, pad], axis=0)
        filtered = jnp.dot(mat[...], operand, preferred_element_type=F32)
        projected[:, at] = (shift + jnp.tanh(BETA * (filtered - ETA))) / quot

    for h in range(2):
        arrived(inner_rows.at[h, three], out_recv.at[h])
        hand(inner_rows.at[h, chip], 2 + h, sib)
    arrived(end_rows.at[three], out_recv.at[4])
    hand(end_rows.at[chip], 6, sib)

    def place_inner(h, which):
        for quarter in range(nx):
            chunk = which * nx + quarter
            design[radius : rows - radius, columns(h, chunk)] = inner_rows[h, chunk]

    def place_ends(which):
        for quarter in range(nx):
            chunk = which * nx + quarter
            for h in range(2):
                design[0:radius, columns(h, chunk)] = end_rows[chunk, h, 0:radius]
                design[rows - radius : rows, columns(h, chunk)] = end_rows[chunk, h, radius:side]

    for h in range(2):
        place_inner(h, core)
    place_ends(core)
    other = pl.ds((1 - core) * nx, nx)
    for h in range(2):
        arrived(inner_rows.at[h, other], out_recv.at[2 + h])
        place_inner(h, 1 - core)
    arrived(end_rows.at[other], out_recv.at[6])
    place_ends(1 - core)

    arrived(pair_in, pair_send.at[0])
    arrived(sum_in, sum_send.at[0])
    arrived(inner_rows.at[:, three], out_send.at[0])
    arrived(inner_rows.at[:, chip], out_send.at[1])
    arrived(end_rows.at[three], out_send.at[2])
    arrived(end_rows.at[chip], out_send.at[3])

    @pl.when(has_down)
    def _():
        arrived(dens_cols.at[:, first_side], dens_send.at[0])
        rows_down.wait_send()
        arrived(edge_in.at[1], edge_send.at[0])

    @pl.when(has_up)
    def _():
        arrived(dens_cols.at[:, first_side], dens_send.at[1])
        rows_up.wait_send()
        arrived(edge_in.at[0], edge_send.at[1])


def write(projected, design, projected_out, design_out, sem):
    count = projected.shape[0] // 4
    for n in range(4):
        at = pl.ds(n * count, count)
        pltpu.make_async_copy(projected.at[at], projected_out.at[at], sem.at[0]).start()
        pltpu.make_async_copy(design.at[at], design_out.at[at], sem.at[1]).start()
    pltpu.make_async_copy(projected, projected_out, sem.at[0]).wait()
    pltpu.make_async_copy(design, design_out, sem.at[1]).wait()


def solution(mesh):
    nka, ndev = mesh.shape["ka"], mesh.shape["dev"]

    def shards(density, fields_fwd, fields_adj, filter_band, k_weights, kpoint_ids):
        rows, cols = density.shape
        taps = filter_band.shape[1]
        radius = (taps - 1) // 2
        nx, width = nka // 2, cols // 2 // nka
        ext_rows = rows + 2 * radius
        in_vmem = pl.BlockSpec(memory_space=pltpu.VMEM)
        dma = pltpu.SemaphoreType.DMA
        results = pl.pallas_call(
            functools.partial(kernel, (nka, ndev, rows, cols, taps)),
            out_shape=[jax.ShapeDtypeStruct((rows, cols), F32)] * 2,
            in_specs=[pl.BlockSpec(memory_space=pltpu.HBM)] * 6,
            out_specs=[in_vmem] * 2,
            scratch_shapes=[
                pltpu.VMEM((2, 6, rows, cols), BF16),
                pltpu.VMEM((2, 2, nx, rows, width), F32),
                pltpu.VMEM((2, nx, rows, width), F32),
                pltpu.VMEM((2, nx, rows, width), F32),
                pltpu.VMEM((2, nx - 1, rows, width), F32),
                pltpu.VMEM((2, nx, 2, radius, width), F32),
                pltpu.VMEM((ext_rows, cols), F32),
                pltpu.VMEM((2, ext_rows + 2 * radius, width), F32),
                pltpu.VMEM((2, taps, 128), F32),
                pltpu.VMEM((256, 128), F32),
                pltpu.VMEM((rows, 256), BF16),
                pltpu.VMEM((ext_rows, 384), BF16),
                pltpu.VMEM((rows, 256), BF16),
                pltpu.VMEM((2 * radius, 256), BF16),
                pltpu.SMEM(k_weights.shape, F32),
                pltpu.SMEM(kpoint_ids.shape, jnp.int32),
                pltpu.VMEM((2, nka, rows - 2 * radius, width), F32),
                pltpu.VMEM((nka, 2, 2 * radius, width), F32),
                dma((4,)),
                dma((5,)),
                pltpu.SemaphoreType.REGULAR((3,)),
                dma((1,)),
                dma((2,)),
                dma((1,)),
                dma((2,)),
                dma((4,)),
                dma((4,)),
                dma((2,)),
                dma((2,)),
                dma((4,)),
                dma((7,)),
            ],
            compiler_params=pltpu.CompilerParams(
                collective_id=0, has_side_effects=True, vmem_limit_bytes=40 * 1024 * 1024
            ),
            name="sensitivities",
        )(
            *(
                pltpu.with_memory_space_constraint(operand, pltpu.HBM)
                for operand in (density, fields_fwd, fields_adj, filter_band.T, k_weights, kpoint_ids)
            )
        )
        return pl.pallas_call(
            write,
            out_shape=[jax.ShapeDtypeStruct((rows, cols), F32)] * 2,
            in_specs=[in_vmem] * 2,
            out_specs=[pl.BlockSpec(memory_space=pltpu.HBM)] * 2,
            scratch_shapes=[dma((2,))],
            name="write_results",
        )(*(pltpu.with_memory_space_constraint(result, pltpu.VMEM) for result in results))

    return jax.shard_map(
        shards,
        mesh=mesh,
        in_specs=(
            P("dev", None),
            P("ka", None, "dev", None),
            P("ka", None, "dev", None),
            P(),
            P(),
            P(),
        ),
        out_specs=(P("dev", None), P("dev", None)),
        check_vma=False,
    )
```

```python
import functools

import jax
import jax.numpy as jnp
from jax import lax
from jax.experimental import pallas as pl
from jax.experimental.pallas import tpu as pltpu
from jax.sharding import PartitionSpec as P

MESH = pl.DeviceIdType.MESH
BETA, ETA = 8.0, 0.5
F32, BF16 = jnp.float32, jnp.bfloat16


def split(value):
    high = value.astype(BF16)
    low = (value - high.astype(F32)).astype(BF16)
    return high, low


def kernel(
    sizes,
    density, fwd, adj, band_t, weights, ids,
    projected, design,
    fields, terms, pair_in, part, sum_in, edge_in,
    ext, dens_cols, band_buf, band_rows, mat, mat_wide, mat_t, mat_edge, weight_buf, id_buf, inner_rows, end_rows,
    load_sem, small_sem, ready, pair_send, pair_recv, sum_send, sum_recv,
    dens_send, dens_recv, edge_send, edge_recv, out_send, out_recv,
):
    nka, ndev, rows, cols, taps = sizes
    radius = (taps - 1) // 2
    nx = nka // 2
    half = cols // 2
    width = half // nka
    ext_rows = rows + 2 * radius
    side = 2 * radius

    ka = lax.axis_index("ka")
    dev = lax.axis_index("dev")
    x, core = ka // 2, lax.rem(ka, 2)
    mine = core * nx + x
    xs = [lax.rem(x + step, nx) for step in range(nx)]
    sib = (x * 2 + 1 - core, dev)
    line = [(xs[step] * 2 + core, dev) for step in range(nx)]
    dev_up, dev_down = lax.rem(dev + 1, ndev), lax.rem(dev + ndev - 1, ndev)
    up = [(xs[step] * 2 + core, dev_up) for step in range(nx)]
    down = [(xs[step] * 2 + core, dev_down) for step in range(nx)]
    has_up, has_down = dev < ndev - 1, dev > 0
    even_up, even_down = has_up & ((dev == 15) | (dev == 31)), has_down & ((dev == 16) | (dev == 32))
    early_up = has_up & (lax.rem(dev, 4) != 3) & (dev != 0)
    early_down = has_down & ((lax.rem(dev, 4) == 0) | (dev == 1)) & ~even_down
    late_up, late_down = has_up & ~early_up, has_down & ~early_down
    late_chip = jnp.where(dev == 0, 0, nx // 2)
    is_late = x == late_chip

    def columns(h, chunk):
        return pl.ds(pl.multiple_of(h * half + chunk * width, width), width)

    def load(src, dst, sem):
        copy = pltpu.make_async_copy(src, dst, sem)
        copy.start()
        return copy

    def arrived(ref, sem):
        pltpu.make_async_copy(ref, ref, sem).wait()

    def chunks(h, which):
        return pl.ds(pl.multiple_of(h * half + which * nx * width, nx * width), nx * width)

    def load_chunks(h, which, sem):
        at = chunks(h, which)
        load(fwd.at[0, :, :, at], fields.at[0, :, :, at], load_sem.at[sem])
        load(adj.at[0, :, :, at], fields.at[1, :, :, at], load_sem.at[sem])

    small = [
        load(weights, weight_buf, small_sem.at[0]),
        load(ids, id_buf, small_sem.at[1]),
    ]
    load_chunks(0, 1 - core, 0)
    load_chunks(0, core, 1)
    load_chunks(1, 1 - core, 2)
    load_chunks(1, core, 3)

    barrier = pltpu.get_barrier_semaphore()

    def greet(semaphore, targets):
        for target in targets:
            pl.semaphore_signal(semaphore, inc=1, device_id=target, device_id_type=MESH)

    greet(barrier, [sib])

    @pl.when(~is_late)
    def _():
        greet(barrier, line[1:])

    @pl.when(early_up | even_up)
    def _():
        greet(barrier, up)

    @pl.when(early_down | even_down)
    def _():
        greet(barrier, down)

    one = jnp.int32(1)
    greeted = nx - 1 + jnp.where(is_late, one, 0) + nx * (jnp.where(late_down, one, 0) + jnp.where(late_up, one, 0))

    def answer():
        @pl.when(late_down & ~even_down)
        def _():
            greet(ready.at[0], down)

        @pl.when(late_up & ~even_up)
        def _():
            greet(ready.at[1], up)

    @pl.when(is_late)
    def _():
        pl.semaphore_wait(barrier, greeted)
        greet(ready.at[2], line[1:])
        answer()

    first_band = lax.max(dev * rows - radius, 0) // 128
    last_band = lax.min((dev * rows - radius + 128) // 128, (ndev * rows - 1) // 128)
    for n, block in enumerate((first_band, last_band)):
        load(band_t.at[:, pl.ds(pl.multiple_of(block * 128, 128), 128)], band_buf.at[n], small_sem.at[2])
    own_rows = pl.ds(side, rows)
    for h in range(2):
        load(density.at[:, columns(h, mine)], dens_cols.at[h, own_rows], small_sem.at[3])
    load_density = load(density, ext.at[pl.ds(radius, rows)], small_sem.at[4])

    def remote(src, dst, send_sem, recv_sem, target):
        return pltpu.make_async_remote_copy(
            src_ref=src, dst_ref=dst, send_sem=send_sem, recv_sem=recv_sem,
            device_id=target, device_id_type=MESH,
        )

    @pl.when(dev == 0)
    def _():
        ext[pl.ds(0, radius)] = jnp.zeros((radius, cols), F32)
        dens_cols[:, pl.ds(0, side)] = jnp.zeros((2, side, width), F32)
        edge_in[0] = jnp.zeros((nx, 2, radius, width), F32)

    @pl.when(dev == ndev - 1)
    def _():
        ext[pl.ds(radius + rows, radius)] = jnp.zeros((radius, cols), F32)
        dens_cols[:, pl.ds(side + rows, side)] = jnp.zeros((2, side, width), F32)
        edge_in[1] = jnp.zeros((nx, 2, radius, width), F32)

    for copy in small:
        copy.wait()
    weight = weight_buf[id_buf[ka]]

    def fill_terms(h, which, sem):
        arrived(fields.at[:, :, :, chunks(h, which)], load_sem.at[sem])
        for quarter in range(nx):
            at = columns(h, which * nx + quarter)
            total = None
            for c in range(6):
                product = fields[0, c, :, at].astype(F32) * fields[1, c, :, at].astype(F32)
                total = product if total is None else total + product if c < 3 else total - product
            terms[h, which, quarter] = weight * total

    pairs = [remote(terms.at[h, 1 - core], pair_in.at[h], pair_send.at[0], pair_recv.at[h], sib) for h in range(2)]
    fill_terms(0, 1 - core, 0)

    @pl.when(~is_late)
    def _():
        pl.semaphore_wait(barrier, greeted)
        answer()

    pairs[0].start()

    first_side, last_side = pl.ds(0, side), pl.ds(rows - side, side)
    cols_down = [
        remote(
            density.at[first_side, columns(h, mine)], dens_cols.at[h, pl.ds(side + rows, side)],
            dens_send.at[0], dens_recv.at[0], down[0],
        )
        for h in range(2)
    ]
    cols_up = [
        remote(
            density.at[last_side, columns(h, mine)], dens_cols.at[h, first_side],
            dens_send.at[1], dens_recv.at[1], up[0],
        )
        for h in range(2)
    ]
    rows_down = remote(
        density.at[pl.ds(0, radius)], ext.at[pl.ds(radius + rows, radius)], dens_send.at[2], dens_recv.at[2], down[0]
    )
    rows_up = remote(
        density.at[pl.ds(rows - radius, radius)], ext.at[pl.ds(0, radius)], dens_send.at[3], dens_recv.at[3], up[0]
    )

    edges_down = [
        remote(part.at[:, xs[s], pl.ds(0, radius)], edge_in.at[1, s], edge_send.at[0], edge_recv.at[0], down[s])
        for s in range(nx)
    ]
    edges_up = [
        remote(
            part.at[:, xs[s], pl.ds(rows - radius, radius)], edge_in.at[0, s],
            edge_send.at[1], edge_recv.at[1], up[s],
        )
        for s in range(nx)
    ]

    @pl.when(late_down)
    def _():
        for copy in cols_down:
            copy.start()

    @pl.when(late_up)
    def _():
        for copy in cols_up:
            copy.start()

    fill_terms(0, core, 1)

    def send_sums(h):
        pairs[h].wait_recv()
        for step in (2, 1, 3, 0):
            part[h, xs[step]] = terms[h, core, xs[step]] + pair_in[h, xs[step]]
            if step:
                copy = remote(
                    part.at[h, xs[step]], sum_in.at[h, step - 1], sum_send.at[0], sum_recv.at[h], line[step]
                )
                pl.when(is_late | (xs[step] != late_chip))(copy.start)

    latest = (dev == 0) & (ka == 0)

    @pl.when(latest)
    def _():
        send_sums(0)

    fill_terms(1, 1 - core, 2)
    pairs[1].start()

    @pl.when(~latest)
    def _():
        send_sums(0)

    fill_terms(1, core, 3)
    send_sums(1)

    @pl.when(late_down)
    def _():
        for copy in edges_down:
            copy.start()

    @pl.when(late_up)
    def _():
        for copy in edges_up:
            copy.start()

    @pl.when(~is_late)
    def _():
        pl.semaphore_wait(ready.at[2], 1)
        slot = lax.rem(late_chip - x + nx, nx) - 1
        for h in range(2):
            remote(
                part.at[h, late_chip], sum_in.at[h, slot], sum_send.at[0], sum_recv.at[h], (late_chip * 2 + core, dev)
            ).start()

    @pl.when(late_down)
    def _():
        rows_down.start()

    @pl.when(late_up)
    def _():
        rows_up.start()

    arrived(band_buf, small_sem.at[2])
    for n in range(2):
        band = band_buf[n]
        band = band / jnp.sum(band, axis=0, keepdims=True)
        band = jnp.concatenate([band, jnp.zeros((128 - taps, 128), F32)], axis=0)
        band_rows[n * 128 : (n + 1) * 128] = band.T
    offset = jnp.where(lax.rem(dev, 2) == 0, 128 - radius, rows - radius)
    band_ext = band_rows[pl.ds(pl.multiple_of(offset, radius), ext_rows), :]

    def shear(value, shift):
        return pltpu.roll(value, shift, 1, stride=1, stride_axis=0)

    def parts_of(value):
        high, low = split(value)
        return high.astype(F32), low.astype(F32)

    high, low = parts_of(shear(band_ext, 0))
    mat_wide[:, 0:128] = high.astype(BF16)
    mat_wide[:, 128:256] = high.astype(BF16)
    mat_wide[:, 256:384] = low.astype(BF16)
    high, low = parts_of(shear(band_ext, 128 - 2 * radius))
    stacked = jnp.concatenate([high, high, low, jnp.zeros((256 - 3 * ext_rows, 128), F32)], axis=0).T
    mat_t[...] = stacked[0:rows].astype(BF16)
    mat_edge[...] = jnp.concatenate([stacked[0:radius], stacked[rows - radius : rows]], axis=0).astype(BF16)
    high, low = parts_of(shear(band_ext[radius : radius + rows], 0))
    mat[:, 0:128] = jnp.concatenate([high[:, :ext_rows], high[:, : 128 - ext_rows]], axis=1).astype(BF16)
    mat[:, 128:256] = jnp.concatenate(
        [high[:, 128 - ext_rows : ext_rows], low[:, :ext_rows], jnp.zeros((rows, 256 - 3 * ext_rows), F32)], axis=1
    ).astype(BF16)

    @pl.when(early_up)
    def _():
        pl.semaphore_wait(ready.at[0], nx)
        for copy in cols_up + edges_up + [rows_up]:
            copy.start()

    @pl.when(early_down)
    def _():
        pl.semaphore_wait(ready.at[1], nx)
        for copy in cols_down + edges_down + [rows_down]:
            copy.start()

    quot = jnp.tanh(jnp.float32(BETA * ETA)) + jnp.tanh(jnp.float32(BETA * (1.0 - ETA)))
    shift = jnp.tanh(jnp.float32(BETA * ETA))
    arrived(dens_cols.at[:, own_rows], small_sem.at[3])
    upper_side = pl.ds(side + rows, side)

    @pl.when(has_down)
    def _():
        arrived(dens_cols.at[:, first_side], dens_recv.at[1])

    @pl.when(has_up)
    def _():
        arrived(dens_cols.at[:, upper_side], dens_recv.at[0])

    high, low = split(jnp.concatenate([dens_cols[0], dens_cols[1]], axis=1))
    gap = jnp.zeros((128 - ext_rows - 2 * radius, 2 * width), BF16)
    operand = jnp.concatenate([high, gap, low, gap, high, gap], axis=0)
    filtered = jnp.dot(mat_wide[...], operand, preferred_element_type=F32)
    inner = jnp.tanh(BETA * (filtered - ETA))
    slope = 11.1 * BETA * (1.0 - inner * inner) / quot

    def transposed(matrix, value):
        high, low = split(value)
        pad = jnp.zeros((256 - 3 * ext_rows, value.shape[1]), BF16)
        return jnp.dot(matrix, jnp.concatenate([high, low, high, pad], axis=0), preferred_element_type=F32)

    def hand(buffer, slot, target):
        remote(buffer, buffer, out_send.at[slot // 2], out_recv.at[slot], target).start()

    chip = pl.ds(core * nx, nx)
    three = pl.ds(0, nx - 1)
    none = jnp.zeros((radius, width), F32)
    grads = []
    for h in range(2):
        arrived(sum_in.at[h], sum_recv.at[h])
        sens = (part[h, x] + sum_in[h, 0]) + (sum_in[h, 1] + sum_in[h, 2])
        grads.append(slope[radius : radius + rows, h * width : (h + 1) * width] * sens)
        own = transposed(mat_t[...], jnp.concatenate([none, grads[h], none], axis=0))
        inner_rows[h, mine] = own[radius : rows - radius]
        for step in (2, 1, 3):
            hand(inner_rows.at[h, mine], h, line[step])

    @pl.when(has_up)
    def _():
        arrived(edge_in.at[1], edge_recv.at[0])

    @pl.when(has_down)
    def _():
        arrived(edge_in.at[0], edge_recv.at[1])

    edge = edge_in[:, 0] + edge_in[:, 1] + (edge_in[:, 2] + edge_in[:, 3])
    first, last = [jnp.concatenate([edge[n, 0], edge[n, 1]], axis=1) for n in range(2)]
    grad = jnp.concatenate(
        [slope[0:radius] * first, jnp.concatenate(grads, axis=1), slope[radius + rows :] * last], axis=0
    )
    ends = transposed(mat_edge[...], grad)
    for h in range(2):
        end_rows[mine, h] = ends[:, h * width : (h + 1) * width]
    for step in (2, 1, 3):
        hand(end_rows.at[mine], 4, line[step])

    load_density.wait()

    @pl.when(has_down)
    def _():
        rows_up.wait_recv()

    @pl.when(has_up)
    def _():
        rows_down.wait_recv()

    for chunk in range(8):
        at = slice(chunk * cols // 8, (chunk + 1) * cols // 8)
        high, low = split(ext[:, at])
        pad = jnp.zeros((256 - 3 * ext_rows, cols // 8), BF16)
        operand = jnp.concatenate([high, low, high, pad], axis=0)
        filtered = jnp.dot(mat[...], operand, preferred_element_type=F32)
        projected[:, at] = (shift + jnp.tanh(BETA * (filtered - ETA))) / quot

    for h in range(2):
        arrived(inner_rows.at[h, three], out_recv.at[h])
        hand(inner_rows.at[h, chip], 2 + h, sib)
    arrived(end_rows.at[three], out_recv.at[4])
    hand(end_rows.at[chip], 6, sib)

    def place_inner(h, which):
        for quarter in range(nx):
            chunk = which * nx + quarter
            design[radius : rows - radius, columns(h, chunk)] = inner_rows[h, chunk]

    def place_ends(which):
        for quarter in range(nx):
            chunk = which * nx + quarter
            for h in range(2):
                design[0:radius, columns(h, chunk)] = end_rows[chunk, h, 0:radius]
                design[rows - radius : rows, columns(h, chunk)] = end_rows[chunk, h, radius:side]

    for h in range(2):
        place_inner(h, core)
    place_ends(core)
    other = pl.ds((1 - core) * nx, nx)
    for h in range(2):
        arrived(inner_rows.at[h, other], out_recv.at[2 + h])
        place_inner(h, 1 - core)
    arrived(end_rows.at[other], out_recv.at[6])
    place_ends(1 - core)

    arrived(pair_in, pair_send.at[0])
    arrived(sum_in, sum_send.at[0])
    arrived(inner_rows.at[:, three], out_send.at[0])
    arrived(inner_rows.at[:, chip], out_send.at[1])
    arrived(end_rows.at[three], out_send.at[2])
    arrived(end_rows.at[chip], out_send.at[3])

    @pl.when(has_down)
    def _():
        arrived(dens_cols.at[:, first_side], dens_send.at[0])
        rows_down.wait_send()
        arrived(edge_in.at[1], edge_send.at[0])

    @pl.when(has_up)
    def _():
        arrived(dens_cols.at[:, first_side], dens_send.at[1])
        rows_up.wait_send()
        arrived(edge_in.at[0], edge_send.at[1])


def write(projected, design, projected_out, design_out, sem):
    count = projected.shape[0] // 4
    for n in range(4):
        at = pl.ds(n * count, count)
        pltpu.make_async_copy(projected.at[at], projected_out.at[at], sem.at[0]).start()
        pltpu.make_async_copy(design.at[at], design_out.at[at], sem.at[1]).start()
    pltpu.make_async_copy(projected, projected_out, sem.at[0]).wait()
    pltpu.make_async_copy(design, design_out, sem.at[1]).wait()


def solution(mesh):
    nka, ndev = mesh.shape["ka"], mesh.shape["dev"]

    def shards(density, fields_fwd, fields_adj, filter_band, k_weights, kpoint_ids):
        rows, cols = density.shape
        taps = filter_band.shape[1]
        radius = (taps - 1) // 2
        nx, width = nka // 2, cols // 2 // nka
        ext_rows = rows + 2 * radius
        in_vmem = pl.BlockSpec(memory_space=pltpu.VMEM)
        dma = pltpu.SemaphoreType.DMA
        results = pl.pallas_call(
            functools.partial(kernel, (nka, ndev, rows, cols, taps)),
            out_shape=[jax.ShapeDtypeStruct((rows, cols), F32)] * 2,
            in_specs=[pl.BlockSpec(memory_space=pltpu.HBM)] * 6,
            out_specs=[in_vmem] * 2,
            scratch_shapes=[
                pltpu.VMEM((2, 6, rows, cols), BF16),
                pltpu.VMEM((2, 2, nx, rows, width), F32),
                pltpu.VMEM((2, nx, rows, width), F32),
                pltpu.VMEM((2, nx, rows, width), F32),
                pltpu.VMEM((2, nx - 1, rows, width), F32),
                pltpu.VMEM((2, nx, 2, radius, width), F32),
                pltpu.VMEM((ext_rows, cols), F32),
                pltpu.VMEM((2, ext_rows + 2 * radius, width), F32),
                pltpu.VMEM((2, taps, 128), F32),
                pltpu.VMEM((256, 128), F32),
                pltpu.VMEM((rows, 256), BF16),
                pltpu.VMEM((ext_rows, 384), BF16),
                pltpu.VMEM((rows, 256), BF16),
                pltpu.VMEM((2 * radius, 256), BF16),
                pltpu.SMEM(k_weights.shape, F32),
                pltpu.SMEM(kpoint_ids.shape, jnp.int32),
                pltpu.VMEM((2, nka, rows - 2 * radius, width), F32),
                pltpu.VMEM((nka, 2, 2 * radius, width), F32),
                dma((4,)),
                dma((5,)),
                pltpu.SemaphoreType.REGULAR((3,)),
                dma((1,)),
                dma((2,)),
                dma((1,)),
                dma((2,)),
                dma((4,)),
                dma((4,)),
                dma((2,)),
                dma((2,)),
                dma((4,)),
                dma((7,)),
            ],
            compiler_params=pltpu.CompilerParams(
                collective_id=0, has_side_effects=True, vmem_limit_bytes=40 * 1024 * 1024
            ),
            name="sensitivities",
        )(
            *(
                pltpu.with_memory_space_constraint(operand, pltpu.HBM)
                for operand in (density, fields_fwd, fields_adj, filter_band.T, k_weights, kpoint_ids)
            )
        )
        return pl.pallas_call(
            write,
            out_shape=[jax.ShapeDtypeStruct((rows, cols), F32)] * 2,
            in_specs=[in_vmem] * 2,
            out_specs=[pl.BlockSpec(memory_space=pltpu.HBM)] * 2,
            scratch_shapes=[dma((2,))],
            name="write_results",
        )(*(pltpu.with_memory_space_constraint(result, pltpu.VMEM) for result in results))

    return jax.shard_map(
        shards,
        mesh=mesh,
        in_specs=(
            P("dev", None),
            P("ka", None, "dev", None),
            P("ka", None, "dev", None),
            P(),
            P(),
            P(),
        ),
        out_specs=(P("dev", None), P("dev", None)),
        check_vma=False,
    )
```

```python
import functools

import jax
import jax.numpy as jnp
from jax import lax
from jax.experimental import pallas as pl
from jax.experimental.pallas import tpu as pltpu
from jax.sharding import PartitionSpec as P

MESH = pl.DeviceIdType.MESH
BETA, ETA = 8.0, 0.5
F32, BF16 = jnp.float32, jnp.bfloat16


def split(value):
    high = value.astype(BF16)
    low = (value - high.astype(F32)).astype(BF16)
    return high, low


def kernel(
    sizes,
    density, fwd, adj, band_t, weights, ids,
    projected, design,
    fields, terms, pair_in, part, sum_in, edge_in,
    ext, dens_cols, band_buf, band_rows, mat, mat_wide, mat_t, mat_edge, weight_buf, id_buf, inner_rows, end_rows,
    load_sem, small_sem, ready, sent, pair_recv, sum_recv, dens_recv, edge_recv, out_recv,
):
    nka, ndev, rows, cols, taps = sizes
    radius = (taps - 1) // 2
    nx = nka // 2
    half = cols // 2
    width = half // nka
    ext_rows = rows + 2 * radius
    side = 2 * radius

    ka = lax.axis_index("ka")
    dev = lax.axis_index("dev")
    x, core = ka // 2, lax.rem(ka, 2)
    mine = core * nx + x
    xs = [lax.rem(x + step, nx) for step in range(nx)]
    sib = (x * 2 + 1 - core, dev)
    line = [(xs[step] * 2 + core, dev) for step in range(nx)]
    dev_up, dev_down = lax.rem(dev + 1, ndev), lax.rem(dev + ndev - 1, ndev)
    up = [(xs[step] * 2 + core, dev_up) for step in range(nx)]
    down = [(xs[step] * 2 + core, dev_down) for step in range(nx)]
    has_up, has_down = dev < ndev - 1, dev > 0
    even_up, even_down = has_up & ((dev == 15) | (dev == 31)), has_down & ((dev == 16) | (dev == 32))
    early_up = has_up & (lax.rem(dev, 4) != 3) & (dev != 0)
    early_down = has_down & ((lax.rem(dev, 4) == 0) | (dev == 1)) & ~even_down
    late_up, late_down = has_up & ~early_up, has_down & ~early_down
    late_chip = jnp.where(dev == 0, 0, nx // 2)
    is_late = x == late_chip

    barrier = pltpu.get_barrier_semaphore()

    def greet(semaphore, targets):
        for target in targets:
            pl.semaphore_signal(semaphore, inc=1, device_id=target, device_id_type=MESH)

    greet(barrier, [sib])

    def columns(h, chunk):
        return pl.ds(pl.multiple_of(h * half + chunk * width, width), width)

    def load(src, dst, sem):
        copy = pltpu.make_async_copy(src, dst, sem)
        copy.start()
        return copy

    def arrived(ref, sem):
        pltpu.make_async_copy(ref, ref, sem).wait()

    def chunks(h, which):
        return pl.ds(pl.multiple_of(h * half + which * nx * width, nx * width), nx * width)

    def load_chunks(h, which, sem):
        at = chunks(h, which)
        load(fwd.at[0, :, :, at], fields.at[0, :, :, at], load_sem.at[sem])
        load(adj.at[0, :, :, at], fields.at[1, :, :, at], load_sem.at[sem])

    load_chunks(0, 1 - core, 0)
    small = [
        load(weights, weight_buf, small_sem.at[0]),
        load(ids, id_buf, small_sem.at[1]),
    ]
    load_chunks(0, core, 1)
    load_chunks(1, 1 - core, 2)
    load_chunks(1, core, 3)

    @pl.when(~is_late)
    def _():
        greet(barrier, line[1:])

    @pl.when(early_up | even_up)
    def _():
        greet(barrier, up)

    @pl.when(early_down | even_down)
    def _():
        greet(barrier, down)

    one = jnp.int32(1)
    greeted = nx - 1 + jnp.where(is_late, one, 0) + nx * (jnp.where(late_down, one, 0) + jnp.where(late_up, one, 0))

    def answer():
        @pl.when(late_down & ~even_down)
        def _():
            greet(ready.at[0], down)

        @pl.when(late_up & ~even_up)
        def _():
            greet(ready.at[1], up)

    @pl.when(is_late)
    def _():
        pl.semaphore_wait(barrier, greeted)
        greet(ready.at[2], line[1:])
        answer()

    first_band = lax.max(dev * rows - radius, 0) // 128
    last_band = lax.min((dev * rows - radius + 128) // 128, (ndev * rows - 1) // 128)
    for n, block in enumerate((first_band, last_band)):
        load(band_t.at[:, pl.ds(pl.multiple_of(block * 128, 128), 128)], band_buf.at[n], small_sem.at[2])
    own_rows = pl.ds(side, rows)
    for h in range(2):
        load(density.at[:, columns(h, mine)], dens_cols.at[h, own_rows], small_sem.at[3])
    load_density = load(density, ext.at[pl.ds(radius, rows)], small_sem.at[4])

    def remote(src, dst, send_sem, recv_sem, target):
        return pltpu.make_async_remote_copy(
            src_ref=src, dst_ref=dst, send_sem=send_sem, recv_sem=recv_sem,
            device_id=target, device_id_type=MESH,
        )

    @pl.when(dev == 0)
    def _():
        ext[pl.ds(0, radius)] = jnp.zeros((radius, cols), F32)
        dens_cols[:, pl.ds(0, side)] = jnp.zeros((2, side, width), F32)
        edge_in[0] = jnp.zeros((nx, 2, radius, width), F32)

    @pl.when(dev == ndev - 1)
    def _():
        ext[pl.ds(radius + rows, radius)] = jnp.zeros((radius, cols), F32)
        dens_cols[:, pl.ds(side + rows, side)] = jnp.zeros((2, side, width), F32)
        edge_in[1] = jnp.zeros((nx, 2, radius, width), F32)

    for copy in small:
        copy.wait()
    weight = weight_buf[id_buf[ka]]

    def fill_terms(h, which, sem):
        arrived(fields.at[:, :, :, chunks(h, which)], load_sem.at[sem])
        for quarter in range(nx):
            at = columns(h, which * nx + quarter)
            total = None
            for c in range(6):
                product = fields[0, c, :, at].astype(F32) * fields[1, c, :, at].astype(F32)
                total = product if total is None else total + product if c < 3 else total - product
            terms[h, which, quarter] = weight * total

    pairs = [remote(terms.at[h, 1 - core], pair_in.at[h], sent.at[0], pair_recv.at[h], sib) for h in range(2)]
    fill_terms(0, 1 - core, 0)

    @pl.when(~is_late)
    def _():
        pl.semaphore_wait(barrier, greeted)
        answer()

    pairs[0].start()

    first_side, last_side = pl.ds(0, side), pl.ds(rows - side, side)
    cols_down = [
        remote(
            density.at[first_side, columns(h, mine)], dens_cols.at[h, pl.ds(side + rows, side)],
            sent.at[2], dens_recv.at[0], down[0],
        )
        for h in range(2)
    ]
    cols_up = [
        remote(
            density.at[last_side, columns(h, mine)], dens_cols.at[h, first_side],
            sent.at[3], dens_recv.at[1], up[0],
        )
        for h in range(2)
    ]
    rows_down = remote(
        density.at[pl.ds(0, radius)], ext.at[pl.ds(radius + rows, radius)], sent.at[2], dens_recv.at[2], down[0]
    )
    rows_up = remote(
        density.at[pl.ds(rows - radius, radius)], ext.at[pl.ds(0, radius)], sent.at[3], dens_recv.at[3], up[0]
    )

    edges_down = [
        remote(part.at[:, xs[s], pl.ds(0, radius)], edge_in.at[1, s], sent.at[2], edge_recv.at[0], down[s])
        for s in range(nx)
    ]
    edges_up = [
        remote(
            part.at[:, xs[s], pl.ds(rows - radius, radius)], edge_in.at[0, s],
            sent.at[3], edge_recv.at[1], up[s],
        )
        for s in range(nx)
    ]

    @pl.when(late_down)
    def _():
        for copy in cols_down:
            copy.start()

    @pl.when(late_up)
    def _():
        for copy in cols_up:
            copy.start()

    fill_terms(0, core, 1)

    def send_sums(h):
        pairs[h].wait_recv()
        for step in (2, 1, 3, 0):
            part[h, xs[step]] = terms[h, core, xs[step]] + pair_in[h, xs[step]]
            if step:
                copy = remote(
                    part.at[h, xs[step]], sum_in.at[h, step - 1], sent.at[1], sum_recv.at[h], line[step]
                )
                pl.when(is_late | (xs[step] != late_chip))(copy.start)

    latest = (dev == 0) & (ka == 0)

    @pl.when(latest)
    def _():
        send_sums(0)

    fill_terms(1, 1 - core, 2)
    pairs[1].start()

    @pl.when(~latest)
    def _():
        send_sums(0)

    fill_terms(1, core, 3)
    send_sums(1)

    @pl.when(late_down)
    def _():
        for copy in edges_down:
            copy.start()

    @pl.when(late_up)
    def _():
        for copy in edges_up:
            copy.start()

    @pl.when(~is_late)
    def _():
        pl.semaphore_wait(ready.at[2], 1)
        slot = lax.rem(late_chip - x + nx, nx) - 1
        for h in range(2):
            remote(
                part.at[h, late_chip], sum_in.at[h, slot], sent.at[1], sum_recv.at[h], (late_chip * 2 + core, dev)
            ).start()

    @pl.when(late_down)
    def _():
        rows_down.start()

    @pl.when(late_up)
    def _():
        rows_up.start()

    arrived(band_buf, small_sem.at[2])
    for n in range(2):
        band = band_buf[n]
        band = band / jnp.sum(band, axis=0, keepdims=True)
        band = jnp.concatenate([band, jnp.zeros((128 - taps, 128), F32)], axis=0)
        band_rows[n * 128 : (n + 1) * 128] = band.T
    offset = jnp.where(lax.rem(dev, 2) == 0, 128 - radius, rows - radius)
    band_ext = band_rows[pl.ds(pl.multiple_of(offset, radius), ext_rows), :]

    def shear(value, shift):
        return pltpu.roll(value, shift, 1, stride=1, stride_axis=0)

    def parts_of(value):
        high, low = split(value)
        return high.astype(F32), low.astype(F32)

    high, low = parts_of(shear(band_ext, 0))
    mat_wide[:, 0:128] = high.astype(BF16)
    mat_wide[:, 128:256] = high.astype(BF16)
    mat_wide[:, 256:384] = low.astype(BF16)
    high, low = parts_of(shear(band_ext, 128 - 2 * radius))
    stacked = jnp.concatenate([high, high, low, jnp.zeros((256 - 3 * ext_rows, 128), F32)], axis=0).T
    mat_t[...] = stacked[0:rows].astype(BF16)
    mat_edge[...] = jnp.concatenate([stacked[0:radius], stacked[rows - radius : rows]], axis=0).astype(BF16)
    high, low = parts_of(shear(band_ext[radius : radius + rows], 0))
    mat[:, 0:128] = jnp.concatenate([high[:, :ext_rows], high[:, : 128 - ext_rows]], axis=1).astype(BF16)
    mat[:, 128:256] = jnp.concatenate(
        [high[:, 128 - ext_rows : ext_rows], low[:, :ext_rows], jnp.zeros((rows, 256 - 3 * ext_rows), F32)], axis=1
    ).astype(BF16)

    @pl.when(early_up)
    def _():
        pl.semaphore_wait(ready.at[0], nx)
        for copy in cols_up + edges_up + [rows_up]:
            copy.start()

    @pl.when(early_down)
    def _():
        pl.semaphore_wait(ready.at[1], nx)
        for copy in cols_down + edges_down + [rows_down]:
            copy.start()

    quot = jnp.tanh(jnp.float32(BETA * ETA)) + jnp.tanh(jnp.float32(BETA * (1.0 - ETA)))
    shift = jnp.tanh(jnp.float32(BETA * ETA))
    arrived(dens_cols.at[:, own_rows], small_sem.at[3])
    upper_side = pl.ds(side + rows, side)

    @pl.when(has_down)
    def _():
        arrived(dens_cols.at[:, first_side], dens_recv.at[1])

    @pl.when(has_up)
    def _():
        arrived(dens_cols.at[:, upper_side], dens_recv.at[0])

    high, low = split(jnp.concatenate([dens_cols[0], dens_cols[1]], axis=1))
    gap = jnp.zeros((128 - ext_rows - 2 * radius, 2 * width), BF16)
    operand = jnp.concatenate([high, gap, low, gap, high, gap], axis=0)
    filtered = jnp.dot(mat_wide[...], operand, preferred_element_type=F32)
    inner = jnp.tanh(BETA * (filtered - ETA))
    slope = 11.1 * BETA * (1.0 - inner * inner) / quot

    def transposed(matrix, value):
        high, low = split(value)
        pad = jnp.zeros((256 - 3 * ext_rows, value.shape[1]), BF16)
        return jnp.dot(matrix, jnp.concatenate([high, low, high, pad], axis=0), preferred_element_type=F32)

    def hand(buffer, slot, target):
        remote(buffer, buffer, sent.at[0 if slot % 4 >= 2 else 1], out_recv.at[slot], target).start()

    chip = pl.ds(core * nx, nx)
    three = pl.ds(0, nx - 1)
    none = jnp.zeros((radius, width), F32)
    grads = []
    for h in range(2):
        arrived(sum_in.at[h], sum_recv.at[h])
        sens = (part[h, x] + sum_in[h, 0]) + (sum_in[h, 1] + sum_in[h, 2])
        grads.append(slope[radius : radius + rows, h * width : (h + 1) * width] * sens)
        own = transposed(mat_t[...], jnp.concatenate([none, grads[h], none], axis=0))
        inner_rows[h, mine] = own[radius : rows - radius]
        for step in (2, 1, 3):
            hand(inner_rows.at[h, mine], h, line[step])

    @pl.when(has_up)
    def _():
        arrived(edge_in.at[1], edge_recv.at[0])

    @pl.when(has_down)
    def _():
        arrived(edge_in.at[0], edge_recv.at[1])

    edge = edge_in[:, 0] + edge_in[:, 1] + (edge_in[:, 2] + edge_in[:, 3])
    first, last = [jnp.concatenate([edge[n, 0], edge[n, 1]], axis=1) for n in range(2)]
    grad = jnp.concatenate(
        [slope[0:radius] * first, jnp.concatenate(grads, axis=1), slope[radius + rows :] * last], axis=0
    )
    ends = transposed(mat_edge[...], grad)
    for h in range(2):
        end_rows[mine, h] = ends[:, h * width : (h + 1) * width]
    for step in (2, 1, 3):
        hand(end_rows.at[mine], 4, line[step])

    load_density.wait()

    @pl.when(has_down)
    def _():
        rows_up.wait_recv()

    @pl.when(has_up)
    def _():
        rows_down.wait_recv()

    for chunk in range(8):
        at = slice(chunk * cols // 8, (chunk + 1) * cols // 8)
        high, low = split(ext[:, at])
        pad = jnp.zeros((256 - 3 * ext_rows, cols // 8), BF16)
        operand = jnp.concatenate([high, low, high, pad], axis=0)
        filtered = jnp.dot(mat[...], operand, preferred_element_type=F32)
        projected[:, at] = (shift + jnp.tanh(BETA * (filtered - ETA))) / quot

    for h in range(2):
        arrived(inner_rows.at[h, three], out_recv.at[h])
        hand(inner_rows.at[h, chip], 2 + h, sib)
    arrived(end_rows.at[three], out_recv.at[4])
    hand(end_rows.at[chip], 6, sib)

    def place_inner(h, which):
        for quarter in range(nx):
            chunk = which * nx + quarter
            design[radius : rows - radius, columns(h, chunk)] = inner_rows[h, chunk]

    def place_ends(which):
        for quarter in range(nx):
            chunk = which * nx + quarter
            for h in range(2):
                design[0:radius, columns(h, chunk)] = end_rows[chunk, h, 0:radius]
                design[rows - radius : rows, columns(h, chunk)] = end_rows[chunk, h, radius:side]

    for h in range(2):
        place_inner(h, core)
    place_ends(core)
    other = pl.ds((1 - core) * nx, nx)
    for h in range(2):
        arrived(inner_rows.at[h, other], out_recv.at[2 + h])
        place_inner(h, 1 - core)
    arrived(end_rows.at[other], out_recv.at[6])
    place_ends(1 - core)

    arrived(terms, sent.at[0])
    arrived(terms.at[:, :, pl.ds(0, nx - 1)], sent.at[1])
    side_bytes = inner_rows.at[:, pl.ds(0, 7), pl.ds(0, 16)]

    @pl.when(has_down)
    def _():
        arrived(side_bytes, sent.at[2])

    @pl.when(has_up)
    def _():
        arrived(side_bytes, sent.at[3])


def write(projected, design, projected_out, design_out, sem):
    count = projected.shape[0] // 4
    for n in range(4):
        at = pl.ds(n * count, count)
        pltpu.make_async_copy(projected.at[at], projected_out.at[at], sem.at[0]).start()
        pltpu.make_async_copy(design.at[at], design_out.at[at], sem.at[1]).start()
    pltpu.make_async_copy(projected, projected_out, sem.at[0]).wait()
    pltpu.make_async_copy(design, design_out, sem.at[1]).wait()


def solution(mesh):
    nka, ndev = mesh.shape["ka"], mesh.shape["dev"]

    def shards(density, fields_fwd, fields_adj, filter_band, k_weights, kpoint_ids):
        rows, cols = density.shape
        taps = filter_band.shape[1]
        radius = (taps - 1) // 2
        nx, width = nka // 2, cols // 2 // nka
        ext_rows = rows + 2 * radius
        in_vmem = pl.BlockSpec(memory_space=pltpu.VMEM)
        dma = pltpu.SemaphoreType.DMA
        results = pl.pallas_call(
            functools.partial(kernel, (nka, ndev, rows, cols, taps)),
            out_shape=[jax.ShapeDtypeStruct((rows, cols), F32)] * 2,
            in_specs=[pl.BlockSpec(memory_space=pltpu.HBM)] * 6,
            out_specs=[in_vmem] * 2,
            scratch_shapes=[
                pltpu.VMEM((2, 6, rows, cols), BF16),
                pltpu.VMEM((2, 2, nx, rows, width), F32),
                pltpu.VMEM((2, nx, rows, width), F32),
                pltpu.VMEM((2, nx, rows, width), F32),
                pltpu.VMEM((2, nx - 1, rows, width), F32),
                pltpu.VMEM((2, nx, 2, radius, width), F32),
                pltpu.VMEM((ext_rows, cols), F32),
                pltpu.VMEM((2, ext_rows + 2 * radius, width), F32),
                pltpu.VMEM((2, taps, 128), F32),
                pltpu.VMEM((256, 128), F32),
                pltpu.VMEM((rows, 256), BF16),
                pltpu.VMEM((ext_rows, 384), BF16),
                pltpu.VMEM((rows, 256), BF16),
                pltpu.VMEM((2 * radius, 256), BF16),
                pltpu.SMEM(k_weights.shape, F32),
                pltpu.SMEM(kpoint_ids.shape, jnp.int32),
                pltpu.VMEM((2, nka, rows - 2 * radius, width), F32),
                pltpu.VMEM((nka, 2, 2 * radius, width), F32),
                dma((4,)),
                dma((5,)),
                pltpu.SemaphoreType.REGULAR((3,)),
                dma((4,)),
                dma((2,)),
                dma((2,)),
                dma((4,)),
                dma((2,)),
                dma((7,)),
            ],
            compiler_params=pltpu.CompilerParams(
                collective_id=0, has_side_effects=True, vmem_limit_bytes=40 * 1024 * 1024
            ),
            name="sensitivities",
        )(
            *(
                pltpu.with_memory_space_constraint(operand, pltpu.HBM)
                for operand in (density, fields_fwd, fields_adj, filter_band.T, k_weights, kpoint_ids)
            )
        )
        return pl.pallas_call(
            write,
            out_shape=[jax.ShapeDtypeStruct((rows, cols), F32)] * 2,
            in_specs=[in_vmem] * 2,
            out_specs=[pl.BlockSpec(memory_space=pltpu.HBM)] * 2,
            scratch_shapes=[dma((2,))],
            name="write_results",
        )(*(pltpu.with_memory_space_constraint(result, pltpu.VMEM) for result in results))

    return jax.shard_map(
        shards,
        mesh=mesh,
        in_specs=(
            P("dev", None),
            P("ka", None, "dev", None),
            P("ka", None, "dev", None),
            P(),
            P(),
            P(),
        ),
        out_specs=(P("dev", None), P("dev", None)),
        check_vma=False,
    )
```
